32 devices in a mesh: parts: 1, ctx: 32 (over z, y, x, core).
Axes of the slice: x: 2, y: 2, z: 4, core: 2. Of those that a mesh axis runs over, the one named last changes fastest.
Arguments:
- hidden_states: bfloat16 [2048, 2880], P(('parts', 'ctx')), may hold values from -6 to 6
- o_proj: bfloat16 [2048, 2880], P('ctx'), may hold values from -1 to 1
- norm_gain: bfloat16 [2880], replicated, may hold values from 0.099609375 to 1.8984375
- router_weight: bfloat16 [2880, 8], replicated, may hold values from -0.109375 to 0.109375
- routes: int32 [2048, 4], P(('parts', 'ctx')), may hold values from 0 to 7, all different within a row; in each aligned block of 64 rows (0 to 63, 64 to 127, ...) at most 36 rows name the same one
- w_gate: bfloat16 [32, 2880, 360], P('ctx'), may hold values from -0.109375 to 0.109375
- w_up: bfloat16 [32, 2880, 360], P('ctx'), may hold values from -0.109375 to 0.109375
- w_down: bfloat16 [32, 360, 2880], P('ctx'), may hold values from -0.15625 to 0.15625
- query: bfloat16 [2048, 2048], P(('parts', 'ctx')), may hold values from -6 to 6
- keys: bfloat16 [2048, 256], P(('parts', 'ctx')), may hold values from -6 to 6
- values: bfloat16 [2048, 256], P(('parts', 'ctx')), may hold values from -6 to 6
Outputs:
- moe_output: bfloat16 [2048, 2880], P(('parts', 'ctx'))
- attended: bfloat16 [2048, 2048], P(('parts', 'ctx'))
The draws below stay inside these ranges and needn't reach their ends.
Inputs may be any that keep to these rules, and one draw needn't show every extreme that they name: `routes`: each row names 4 different experts; the rows of one device name no expert more than 36 times, and in every draw some device names some expert exactly 36 times.
All inputs are finite; a program needn't handle non-finite values.
Results may differ from the reference program's by a relative error of at most 0.012.
Values may be sent and summed in bfloat16 or wider, within the bound.
A program may use at most 128 MiB of HBM per device.

```python
import math
import jax
import jax.numpy as jnp
import numpy as np
from jax import lax

D = 2880
HEADS = 32
KV_HEADS = 4
HEAD_DIM = 64
FF = 1440
SPLIT = 4
TOP = 4
TOK_DEV = 64
FF_DEV = 360
EXPERTS = 8
CAP = 36
TOKENS = 2048
N_CTX = 32


def draw_query(key, part):
    key = jax.random.fold_in(key, 11)
    result = jnp.clip(jax.random.normal(key, (TOKENS, HEADS * HEAD_DIM), jnp.float32), -6.0, 6.0)
    return result.astype(jnp.bfloat16)


def draw_keys(key, part):
    key = jax.random.fold_in(key, 23)
    result = jnp.clip(jax.random.normal(key, (TOKENS, KV_HEADS * HEAD_DIM), jnp.float32), -6.0, 6.0)
    return result.astype(jnp.bfloat16)


def block_scale(stream_key, extent, shards, least, top_value):
    level, own = 1.0, jax.random.fold_in(stream_key, 6)
    for axis_at, parts in shards:
        steps = jnp.exp(jax.random.uniform(jax.random.fold_in(own, axis_at), (parts,), jnp.float32, least / len(shards), top_value / len(shards)))
        level = level * jnp.repeat(steps, extent[axis_at] // parts).reshape([-1 if axis == axis_at else 1 for axis in range(len(extent))])
    return level


def routed_block(rng, own, number, rows, amount, top, bound, lean):
    sequence = jax.random.permutation(rng, amount)
    crowded, ordinary = shares(amount, rows * top, bound, lean, True), shares(amount, rows * top, bound, lean, False)
    places = jnp.arange(amount)

    def named(lengths, offset_by):
        used = int((lengths > 0).sum())
        fixed = max(1, used // 4)
        moved = fixed + (places - fixed + offset_by * (used - fixed)) % max(1, amount - fixed)
        return jnp.zeros((amount,), jnp.int32).at[sequence[jnp.where(places < fixed, places, moved)]].set(jnp.asarray(lengths, jnp.int32))

    lengths = jnp.where(number % 4 == 0, named(crowded, number // 4), named(ordinary, number - number // 4 - 1))
    mixed = jax.random.permutation(jax.random.fold_in(own, 3), amount)
    giver, taker = mixed[0:amount // 2 * 2:2], mixed[1:amount // 2 * 2:2]
    slack = jnp.minimum(lengths[giver] - 1, bound - lengths[taker]) // 2
    slack = jnp.where((giver == sequence[0]) | (taker == sequence[0]) | (lengths[taker] == 0), 0, jnp.maximum(slack, 0))
    moved = jax.random.randint(jax.random.fold_in(own, 4), (amount // 2,), 0, 1 << 20) % (slack + 1)
    lengths = lengths.at[giver].add(-moved).at[taker].add(moved)
    labels = jnp.searchsorted(jnp.cumsum(lengths), jnp.arange(rows * top), side="right").astype(jnp.int32)
    listing = labels.reshape(top, rows).T
    listing = listing[jax.random.permutation(jax.random.fold_in(own, 1), rows)]
    offset_by = jax.random.randint(jax.random.fold_in(own, 2), (rows, 1), 0, top)
    return jnp.take_along_axis(listing, (jnp.arange(top)[None, :] + offset_by) % top, axis=1)


def shares(count, total, most, lean, full):
    weights = [(1 << 20) // math.isqrt(rank ** lean) + 1 for rank in range(1, count + 1)]
    largest = most if full else min(most, max(-(-total // count), total * weights[0] // sum(weights)))
    least = 1 if total - largest >= count - 1 else 0
    counts, rest = [largest] + [least] * (count - 1), total - largest - least * (count - 1)
    while rest > 0:
        candidates = [i for i in range(1, count) if counts[i] < largest] or [i for i in range(1, count) if counts[i] < most]
        whole, budget = sum([weights[i] for i in candidates]), rest
        for i in candidates:
            more = min(most - counts[i], max(1, budget * weights[i] // whole), rest)
            counts[i] = counts[i] + more
            rest = rest - more
    return np.array(counts)


def noise(own_key, extent, scale, reach, shards=(), kind=jnp.bfloat16):
    drawn = jax.random.normal(own_key, extent, jnp.float32) * scale
    if len(shards) > 0:
        drawn = block_scale(own_key, extent, shards, -0.22, 0.18) * drawn
    return jnp.clip(drawn, min=-reach, max=reach).astype(kind)


def setup_inputs(seed: int = 0, part: int = 0) -> dict:
    seeds = jax.random.split(jax.random.key(seed), 12)
    part_splits = jax.random.split(jax.random.fold_in(seeds[11], part), 12)
    hidden_states = noise(part_splits[0], (TOKENS, D), 1.0, 6.0, ((0, 32),))
    o_proj = noise(seeds[1], (HEADS * HEAD_DIM, D), (HEADS * HEAD_DIM // 64) ** -0.5, 1.0, ((0, 32),))
    norm_gain = jnp.clip(1.0 + 0.18 * jax.random.normal(seeds[2], (D,), jnp.float32), 0.099609375, 1.8984375).astype(jnp.bfloat16)
    router_weight = noise(seeds[3], (D, EXPERTS), D ** -0.5, 0.109375)
    routes_keys = jax.random.split(jax.random.fold_in(part_splits[4], 1), TOKENS // TOK_DEV)
    routes_turns = jax.random.permutation(jax.random.fold_in(part_splits[4], 3), TOKENS // TOK_DEV)
    routes = jax.vmap(lambda own, number: routed_block(jax.random.fold_in(part_splits[4], 2), own, number, TOK_DEV, EXPERTS, TOP, CAP, 0))(routes_keys, routes_turns).reshape((TOKENS, TOP))
    w_gate = noise(seeds[5], (N_CTX, D, FF_DEV), D ** -0.5, 0.109375, ((0, 32),))
    w_up = noise(seeds[6], (N_CTX, D, FF_DEV), D ** -0.5, 0.109375, ((0, 32),))
    w_down = noise(seeds[7], (N_CTX, FF_DEV, D), FF ** -0.5, 0.15625, ((0, 32),))
    query = draw_query(jax.random.fold_in(jax.random.fold_in(seeds[11], part), 71), part)
    keys = draw_keys(jax.random.fold_in(jax.random.fold_in(seeds[11], part), 71), part)
    values = noise(part_splits[10], (TOKENS, KV_HEADS * HEAD_DIM), 1.0, 6.0, ((0, 32),))
    return {"hidden_states": hidden_states, "o_proj": o_proj, "norm_gain": norm_gain, "router_weight": router_weight, "routes": routes, "w_gate": w_gate, "w_up": w_up, "w_down": w_down, "query": query, "keys": keys, "values": values}


def attend_block(query_rows, key_rows, value_rows, span):
    group_size = HEADS // KV_HEADS
    queries = query_rows.astype(jnp.float32).reshape(TOK_DEV, KV_HEADS, group_size, HEAD_DIM)
    key_grid = key_rows.astype(jnp.float32).reshape(4 * TOK_DEV, KV_HEADS, HEAD_DIM)
    value_grid = value_rows.astype(jnp.float32).reshape(4 * TOK_DEV, KV_HEADS, HEAD_DIM)
    scores = jnp.einsum('tgrd,pgd->grtp', queries, key_grid) * HEAD_DIM ** (-0.5)
    query_pos = span * TOK_DEV + jnp.arange(TOK_DEV, dtype=jnp.int32)
    key_pos = (span - 3) * TOK_DEV + jnp.arange(4 * TOK_DEV, dtype=jnp.int32)
    allowed = (key_pos[None, :] >= 0) & (key_pos[None, :] <= query_pos[:, None])
    scores = jnp.where(allowed, scores, -1e+30)
    top_score = lax.optimization_barrier(jnp.max(scores, axis=-1, keepdims=True))
    weights = jnp.where(allowed, jnp.exp(scores - top_score), 0.0)
    probs = (weights / lax.optimization_barrier(jnp.sum(weights, axis=-1, keepdims=True))).astype(jnp.bfloat16)
    mixed_heads = jnp.einsum('grtp,pgd->tgrd', probs.astype(jnp.float32), value_grid)
    return mixed_heads.reshape(TOK_DEV, HEADS * HEAD_DIM).astype(jnp.bfloat16)

def reference(hidden_states, o_proj, norm_gain, router_weight, routes, w_gate, w_up, w_down, query, keys, values):
    padded_keys = jnp.concatenate([jnp.zeros((3 * TOK_DEV, KV_HEADS * HEAD_DIM), keys.dtype), keys], axis=0)
    padded_values = jnp.concatenate([jnp.zeros((3 * TOK_DEV, KV_HEADS * HEAD_DIM), values.dtype), values], axis=0)

    def one_span(span):
        start = (span * TOK_DEV).astype(jnp.int32)
        query_rows = lax.dynamic_slice_in_dim(query, start, TOK_DEV, 0)
        key_rows = lax.dynamic_slice_in_dim(padded_keys, start, 4 * TOK_DEV, 0)
        value_rows = lax.dynamic_slice_in_dim(padded_values, start, 4 * TOK_DEV, 0)
        return attend_block(query_rows, key_rows, value_rows, span)
    attended = lax.map(one_span, jnp.arange(N_CTX, dtype=jnp.int32)).reshape(TOKENS, HEADS * HEAD_DIM)
    projected = jnp.dot(attended, o_proj, preferred_element_type=jnp.float32)
    stream = (hidden_states.astype(jnp.float32) + projected).astype(jnp.bfloat16)
    features = stream.astype(jnp.float32)
    normed = (features * lax.rsqrt(lax.optimization_barrier(jnp.mean(features * features, axis=-1, keepdims=True)) + 1e-05) * norm_gain.astype(jnp.float32)).astype(jnp.bfloat16)
    logits = jnp.dot(normed, router_weight, preferred_element_type=jnp.float32)
    picked = jnp.take_along_axis(logits, routes, axis=1)
    route_weight = jax.nn.softmax(picked, axis=-1)
    flat_expert = routes.reshape(-1)
    flat_token = jnp.arange(TOKENS * TOP, dtype=jnp.int32) // TOP
    flat_weight = route_weight.reshape(-1)
    most_rows = N_CTX * CAP

    def one_expert(total, expert):
        order = jnp.argsort((flat_expert != expert).astype(jnp.int32), stable=True)[:most_rows].astype(jnp.int32)
        valid = flat_expert[order] == expert
        tokens_of = flat_token[order]
        rows = normed[tokens_of]
        summed = jnp.zeros((most_rows, D), jnp.float32)
        for shard in range(SPLIT):
            index = (expert * SPLIT + shard).astype(jnp.int32)
            gate_val = jnp.dot(rows, lax.dynamic_index_in_dim(w_gate, index, 0, keepdims=False), preferred_element_type=jnp.float32)
            up_val = jnp.dot(rows, lax.dynamic_index_in_dim(w_up, index, 0, keepdims=False), preferred_element_type=jnp.float32)
            activated = ((up_val + 1.0) * gate_val * jax.nn.sigmoid(1.702 * gate_val)).astype(jnp.bfloat16)
            piece = jnp.dot(activated, lax.dynamic_index_in_dim(w_down, index, 0, keepdims=False), preferred_element_type=jnp.float32).astype(jnp.bfloat16)
            summed = summed + piece.astype(jnp.float32)
        expert_sum = lax.optimization_barrier(summed.astype(jnp.bfloat16)).astype(jnp.float32)
        scale_rows = jnp.where(valid, flat_weight[order], 0.0)
        total = total.at[tokens_of].add(expert_sum * scale_rows[:, None])
        return (total, None)
    experts_sum, _unused = lax.scan(one_expert, jnp.zeros((TOKENS, D), jnp.float32), jnp.arange(EXPERTS, dtype=jnp.int32))
    moe_output = (features + experts_sum).astype(jnp.bfloat16)
    return (moe_output, attended)
```

```python
import functools

import jax
import jax.numpy as jnp
from jax import lax
from jax.experimental import pallas as pl
from jax.experimental.pallas import tpu as pltpu
from jax.sharding import PartitionSpec as P

HEADS = 32
KV_HEADS = 4
HEAD_DIM = 64


def from_behind(block, axis, distance):
    devices = range(lax.axis_size(axis))
    route = [(i - distance, i) for i in devices if i - distance in devices]
    return lax.ppermute(block, axis, route)


def attend_block(query_rows, key_rows, value_rows, span, tok_rows):
    group_size = HEADS // KV_HEADS
    queries = query_rows.reshape(tok_rows, KV_HEADS, group_size, HEAD_DIM)
    key_grid = key_rows.reshape(4 * tok_rows, KV_HEADS, HEAD_DIM)
    value_grid = value_rows.reshape(4 * tok_rows, KV_HEADS, HEAD_DIM)
    scores = jnp.einsum(
        "tgrd,pgd->grtp", queries, key_grid, preferred_element_type=jnp.float32
    ) * HEAD_DIM ** (-0.5)
    query_pos = span * tok_rows + jnp.arange(tok_rows, dtype=jnp.int32)
    key_pos = (span - 3) * tok_rows + jnp.arange(4 * tok_rows, dtype=jnp.int32)
    allowed = (key_pos[None, :] >= 0) & (key_pos[None, :] <= query_pos[:, None])
    scores = jnp.where(allowed, scores, -1e30)
    top_score = jnp.max(scores, axis=-1, keepdims=True)
    weights = jnp.where(allowed, jnp.exp(scores - top_score), 0.0)
    probs = (weights / jnp.sum(weights, axis=-1, keepdims=True)).astype(jnp.bfloat16)
    mixed_heads = jnp.einsum(
        "grtp,pgd->tgrd", probs, value_grid, preferred_element_type=jnp.float32
    )
    return mixed_heads.reshape(tok_rows, HEADS * HEAD_DIM).astype(jnp.bfloat16)


MEMBERS = 4


def expert_kernel(
    groups,
    slab_ref,
    gate_hbm,
    up_hbm,
    down_hbm,
    out_ref,
    recv,
    pieces,
    near,
    pair_sum,
    far,
    final,
    gate_ref,
    up_ref,
    down_ref,
    weight_sem,
    send_sem,
    recv_sem,
):
    me = lax.axis_index("ctx")
    group = me // MEMBERS
    j = me % MEMBERS
    j_sib = j + 1 - 2 * (j % 2)
    j_far = (j + 2) % MEMBERS
    j_diag = MEMBERS - 1 - j
    sibling = group * MEMBERS + j_sib
    partner = group * MEMBERS + j_far

    def to(src, dst, kind, here, there, device):
        return pltpu.make_async_remote_copy(
            src_ref=src,
            dst_ref=dst,
            send_sem=send_sem.at[kind, here],
            recv_sem=recv_sem.at[kind, there],
            device_id={"ctx": device},
            device_id_type=pl.DeviceIdType.MESH,
        )

    weight_copies = [
        pltpu.make_async_copy(src, dst, weight_sem.at[i])
        for i, (src, dst) in enumerate(
            ((gate_hbm.at[0], gate_ref), (up_hbm.at[0], up_ref), (down_hbm.at[0], down_ref))
        )
    ]
    for copy in weight_copies:
        copy.start()

    barrier = pltpu.get_barrier_semaphore()

    def greet(device):
        pl.semaphore_signal(
            barrier, inc=1, device_id={"ctx": device}, device_id_type=pl.DeviceIdType.MESH
        )

    @pl.loop(1, groups)
    def _(o):
        greet(lax.rem(group + o, groups) * MEMBERS + j)

    greet(sibling)
    greet(partner)
    pl.semaphore_wait(barrier, groups + 1)

    def scatter(target):
        return to(
            slab_ref.at[target], recv.at[group, j], 0, target, group, target * MEMBERS + j
        )

    def scattered(s):
        return to(slab_ref.at[s], recv.at[s, j], 0, s, s, sibling)

    def share_sibling(s):
        return to(recv.at[s, j], recv.at[s, j], 1, s, s, sibling)

    def share_partner(s):
        return to(recv.at[s, j], recv.at[s, j], 2, s, s, partner)

    def share_diag(s):
        return to(recv.at[s, j_far], recv.at[s, j_far], 3, s, s, sibling)

    def piece_near(s):
        return to(pieces.at[s, j_sib], near.at[s, 0], 4, s, s, sibling)

    def piece_diag(s):
        return to(pieces.at[s, j_diag], near.at[s, 1], 5, s, s, sibling)

    def piece_far(s):
        return to(pair_sum.at[s], far.at[s], 6, s, s, partner)

    def give_back(s):
        return to(final.at[s], out_ref.at[group], 7, s, group, s * MEMBERS + j)

    def given_back(s):
        return to(final.at[s], out_ref.at[s], 7, s, s, s * MEMBERS + j)

    @pl.loop(1, groups)
    def _(o):
        scatter(lax.rem(group + o, groups)).start()

    recv[group, j] = slab_ref[group]

    def source(step):
        return lax.rem(group - step + groups, groups)

    rows, width = recv.shape[2], recv.shape[3]

    @pl.loop(0, groups + 4)
    def _(t):
        @pl.when(t < groups)
        def _():
            s = source(t)

            @pl.when(t > 0)
            def _():
                scattered(s).wait_recv()

            share_partner(s).start()
            share_sibling(s).start()

        @pl.when((t >= 1) & (t < groups + 1))
        def _():
            s = source(t - 1)
            share_partner(s).wait_recv()
            share_diag(s).start()

        @pl.when((t >= 4) & (t < groups + 4))
        def _():
            s = source(t - 4)
            piece_far(s).wait_recv()
            total = (
                pieces[s, j].astype(jnp.float32)
                + near[s, 0].astype(jnp.float32)
                + far[s].astype(jnp.float32)
            ).astype(jnp.bfloat16)

            @pl.when(t == 4)
            def _():
                out_ref[group] = total

            @pl.when(t > 4)
            def _():
                final[s] = total
                give_back(s).start()

        @pl.when((t >= 3) & (t < groups + 3))
        def _():
            s = source(t - 3)
            piece_near(s).wait_recv()
            piece_diag(s).wait_recv()
            pair_sum[s] = (
                pieces[s, j_far].astype(jnp.float32) + near[s, 1].astype(jnp.float32)
            ).astype(jnp.bfloat16)
            piece_far(s).start()

        @pl.when((t >= 2) & (t < groups + 2))
        def _():
            s = source(t - 2)

            @pl.when(t == 2)
            def _():
                for copy in weight_copies:
                    copy.wait()

            share_sibling(s).wait_recv()
            share_diag(s).wait_recv()
            block = recv[s].reshape(MEMBERS * rows, width)
            gate = jnp.dot(block, gate_ref[...], preferred_element_type=jnp.float32)
            up = jnp.dot(block, up_ref[...], preferred_element_type=jnp.float32)
            activated = ((up + 1.0) * gate * jax.nn.sigmoid(1.702 * gate)).astype(jnp.bfloat16)
            for at in range(0, width, 768):
                span = slice(at, min(at + 768, width))
                piece = jnp.dot(
                    activated, down_ref[:, span], preferred_element_type=jnp.float32
                ).astype(jnp.bfloat16)
                pieces[s, :, :, span] = piece.reshape(MEMBERS, rows, span.stop - span.start)
            piece_near(s).start()
            piece_diag(s).start()

    @pl.loop(0, groups)
    def _(s):
        share_sibling(s).wait_send()
        share_partner(s).wait_send()
        share_diag(s).wait_send()
        piece_near(s).wait_send()
        piece_diag(s).wait_send()
        piece_far(s).wait_send()

    @pl.loop(1, groups)
    def _(o):
        s = source(o)
        scattered(s).wait_send()
        given_back(s).wait_send()
        given_back(s).wait_recv()


def experts_call(slabs, w_gate, w_up, w_down):
    groups, slots, width = slabs.shape
    hidden = w_gate.shape[2]
    anywhere = pl.BlockSpec(memory_space=pl.ANY)
    vmem = pl.BlockSpec(memory_space=pltpu.VMEM)

    def buffer(*shape):
        return pltpu.VMEM(shape, jnp.bfloat16)

    return pl.pallas_call(
        functools.partial(expert_kernel, groups),
        out_shape=jax.ShapeDtypeStruct(slabs.shape, jnp.bfloat16),
        in_specs=[vmem, anywhere, anywhere, anywhere],
        out_specs=vmem,
        scratch_shapes=[
            buffer(groups, MEMBERS, slots, width),
            buffer(groups, MEMBERS, slots, width),
            buffer(groups, 2, slots, width),
            buffer(groups, slots, width),
            buffer(groups, slots, width),
            buffer(groups, slots, width),
            buffer(width, hidden),
            buffer(width, hidden),
            buffer(hidden, width),
            pltpu.SemaphoreType.DMA((3,)),
            pltpu.SemaphoreType.DMA((8, groups)),
            pltpu.SemaphoreType.DMA((8, groups)),
        ],
        compiler_params=pltpu.CompilerParams(
            collective_id=0, has_side_effects=True, vmem_limit_bytes=56 * 1024 * 1024
        ),
    )(slabs, w_gate, w_up, w_down)


def local(
    hidden_states,
    o_proj,
    norm_gain,
    router_weight,
    routes,
    w_gate,
    w_up,
    w_down,
    query,
    keys,
    values,
):
    tok_rows = hidden_states.shape[0]
    model_width = hidden_states.shape[1]
    per_token = routes.shape[1]
    experts = router_weight.shape[1]
    devices = lax.axis_size("ctx")
    shard_count = devices // experts
    capacity = min(tok_rows, (tok_rows * per_token // experts // shard_count + 1) * shard_count)
    slots = -(-capacity // 8) * 8
    span = lax.axis_index("ctx")
    kv_pair = jnp.stack([keys, values])
    pieces = [kv_pair]
    current = kv_pair
    for step_index in range(3):
        current = from_behind(current, "ctx", 1)
        pieces.append(current)
    window = jnp.concatenate(pieces[::-1], axis=1)
    attended = attend_block(query, window[0], window[1], span, tok_rows)
    projected = jnp.dot(
        attended,
        lax.all_gather(o_proj, "ctx", axis=0, tiled=True),
        preferred_element_type=jnp.float32,
    )
    stream = (hidden_states.astype(jnp.float32) + projected).astype(jnp.bfloat16)
    features = stream.astype(jnp.float32)
    normed = (
        features
        * lax.rsqrt(jnp.mean(features * features, axis=-1, keepdims=True) + 1e-05)
        * norm_gain.astype(jnp.float32)
    ).astype(jnp.bfloat16)
    logits = jnp.dot(normed, router_weight, preferred_element_type=jnp.float32)
    choices = jnp.arange(experts, dtype=jnp.int32)
    named = jnp.any(routes[:, :, None] == choices, axis=1)
    top_logit = jnp.max(jnp.where(named, logits, -jnp.inf), axis=-1, keepdims=True)
    raw = jnp.where(named, jnp.exp(jnp.where(named, logits - top_logit, 0.0)), 0.0)
    route_weight = raw / jnp.sum(raw, axis=-1, keepdims=True)
    tokens = jnp.arange(tok_rows, dtype=jnp.int32)
    earlier = (tokens[None, :] < tokens[:, None]).astype(jnp.bfloat16)
    rank = jnp.dot(earlier, named.astype(jnp.bfloat16), preferred_element_type=jnp.float32)
    slot_index = jnp.arange(slots, dtype=jnp.int32)
    assign = named[:, :, None] & (rank.astype(jnp.int32)[:, :, None] == slot_index)
    place = assign.astype(jnp.bfloat16).reshape(tok_rows, experts * slots)
    slabs = lax.dot_general(
        place, normed, (((0,), (0,)), ((), ())), preferred_element_type=jnp.float32
    ).astype(jnp.bfloat16).reshape(experts, slots, model_width)
    summed = experts_call(slabs, w_gate, w_up, w_down).reshape(experts * slots, model_width)
    weights = jnp.where(assign, route_weight[:, :, None], 0.0).reshape(tok_rows, experts * slots)
    upper = weights.astype(jnp.bfloat16)
    lower = (weights - upper.astype(jnp.float32)).astype(jnp.bfloat16)
    both = jnp.dot(
        jnp.concatenate([upper, lower]), summed, preferred_element_type=jnp.float32
    )
    moe_output = (features + both[:tok_rows] + both[tok_rows:]).astype(jnp.bfloat16)
    return (moe_output, attended)


def solution(mesh):
    in_specs = (
        P(("parts", "ctx"), None),
        P("ctx", None),
        P(),
        P(),
        P(("parts", "ctx"), None),
        P("ctx", None, None),
        P("ctx", None, None),
        P("ctx", None, None),
        P(("parts", "ctx"), None),
        P(("parts", "ctx"), None),
        P(("parts", "ctx"), None),
    )
    out_specs = (P(("parts", "ctx"), None), P(("parts", "ctx"), None))
    return jax.shard_map(local, mesh=mesh, in_specs=in_specs, out_specs=out_specs, check_vma=False)
```

```python
import functools

import jax
import jax.numpy as jnp
from jax import lax
from jax.experimental import pallas as pl
from jax.experimental.pallas import tpu as pltpu
from jax.sharding import PartitionSpec as P

HEADS = 32
KV_HEADS = 4
HEAD_DIM = 64


MEMBERS = 4


def expert_kernel(
    groups,
    slab_ref,
    gate_hbm,
    up_hbm,
    down_hbm,
    out_ref,
    recv,
    pieces,
    near,
    pair_sum,
    far,
    final,
    gate_ref,
    up_ref,
    down_ref,
    weight_sem,
    send_sem,
    recv_sem,
):
    me = lax.axis_index("ctx")
    group = me // MEMBERS
    j = me % MEMBERS
    j_sib = j + 1 - 2 * (j % 2)
    j_far = (j + 2) % MEMBERS
    j_diag = MEMBERS - 1 - j
    sibling = group * MEMBERS + j_sib
    partner = group * MEMBERS + j_far

    def to(src, dst, kind, here, there, device):
        return pltpu.make_async_remote_copy(
            src_ref=src,
            dst_ref=dst,
            send_sem=send_sem.at[kind, here],
            recv_sem=recv_sem.at[kind, there],
            device_id={"ctx": device},
            device_id_type=pl.DeviceIdType.MESH,
        )

    weight_copies = [
        pltpu.make_async_copy(src, dst, weight_sem.at[i])
        for i, (src, dst) in enumerate(
            ((gate_hbm.at[0], gate_ref), (up_hbm.at[0], up_ref), (down_hbm.at[0], down_ref))
        )
    ]
    for copy in weight_copies:
        copy.start()

    barrier = pltpu.get_barrier_semaphore()

    def greet(device):
        pl.semaphore_signal(
            barrier, inc=1, device_id={"ctx": device}, device_id_type=pl.DeviceIdType.MESH
        )

    @pl.loop(1, groups)
    def _(o):
        greet(lax.rem(group + o, groups) * MEMBERS + j)

    greet(sibling)
    greet(partner)
    pl.semaphore_wait(barrier, groups + 1)

    def scatter(target):
        return to(
            slab_ref.at[target], recv.at[group, j], 0, target, group, target * MEMBERS + j
        )

    def scattered(s):
        return to(slab_ref.at[s], recv.at[s, j], 0, s, s, sibling)

    def share_sibling(s):
        return to(recv.at[s, j], recv.at[s, j], 1, s, s, sibling)

    def share_partner(s):
        return to(recv.at[s, j], recv.at[s, j], 2, s, s, partner)

    def share_diag(s):
        return to(recv.at[s, j_far], recv.at[s, j_far], 3, s, s, sibling)

    def piece_near(s):
        return to(pieces.at[s, j_sib], near.at[s, 0], 4, s, s, sibling)

    def piece_diag(s):
        return to(pieces.at[s, j_diag], near.at[s, 1], 5, s, s, sibling)

    def piece_far(s):
        return to(pair_sum.at[s], far.at[s], 6, s, s, partner)

    def give_back(s):
        return to(final.at[s], out_ref.at[group], 7, s, group, s * MEMBERS + j)

    def given_back(s):
        return to(final.at[s], out_ref.at[s], 7, s, s, s * MEMBERS + j)

    @pl.loop(1, groups)
    def _(o):
        scatter(lax.rem(group + o, groups)).start()

    recv[group, j] = slab_ref[group]

    def source(step):
        return lax.rem(group - step + groups, groups)

    rows, width = recv.shape[2], recv.shape[3]

    @pl.loop(0, groups + 4)
    def _(t):
        @pl.when(t < groups)
        def _():
            s = source(t)

            @pl.when(t > 0)
            def _():
                scattered(s).wait_recv()

            share_partner(s).start()
            share_sibling(s).start()

        @pl.when((t >= 1) & (t < groups + 1))
        def _():
            s = source(t - 1)
            share_partner(s).wait_recv()
            share_diag(s).start()

        @pl.when((t >= 4) & (t < groups + 4))
        def _():
            s = source(t - 4)
            piece_far(s).wait_recv()
            total = (
                pieces[s, j].astype(jnp.float32)
                + near[s, 0].astype(jnp.float32)
                + far[s].astype(jnp.float32)
            ).astype(jnp.bfloat16)

            @pl.when(t == 4)
            def _():
                out_ref[group] = total

            @pl.when(t > 4)
            def _():
                final[s] = total
                give_back(s).start()

        @pl.when((t >= 3) & (t < groups + 3))
        def _():
            s = source(t - 3)
            piece_near(s).wait_recv()
            piece_diag(s).wait_recv()
            pair_sum[s] = (
                pieces[s, j_far].astype(jnp.float32) + near[s, 1].astype(jnp.float32)
            ).astype(jnp.bfloat16)
            piece_far(s).start()

        @pl.when((t >= 2) & (t < groups + 2))
        def _():
            s = source(t - 2)

            @pl.when(t == 2)
            def _():
                for copy in weight_copies:
                    copy.wait()

            share_sibling(s).wait_recv()
            share_diag(s).wait_recv()
            block = recv[s].reshape(MEMBERS * rows, width)
            across = (((1,), (1,)), ((), ()))
            gate = lax.dot_general(
                block, gate_ref[...], across, preferred_element_type=jnp.float32
            )
            up = lax.dot_general(block, up_ref[...], across, preferred_element_type=jnp.float32)
            activated = ((up + 1.0) * gate * jax.nn.sigmoid(1.702 * gate)).astype(jnp.bfloat16)
            for at in range(0, width, 768):
                span = slice(at, min(at + 768, width))
                piece = jnp.dot(
                    activated, down_ref[:, span], preferred_element_type=jnp.float32
                ).astype(jnp.bfloat16)
                pieces[s, :, :, span] = piece.reshape(MEMBERS, rows, span.stop - span.start)
            piece_near(s).start()
            piece_diag(s).start()

    @pl.loop(0, groups)
    def _(s):
        share_sibling(s).wait_send()
        share_partner(s).wait_send()
        share_diag(s).wait_send()
        piece_near(s).wait_send()
        piece_diag(s).wait_send()
        piece_far(s).wait_send()

    @pl.loop(1, groups)
    def _(o):
        s = source(o)
        scattered(s).wait_send()
        given_back(s).wait_send()
        given_back(s).wait_recv()


def experts_call(slabs, w_gate, w_up, w_down):
    groups, slots, width = slabs.shape
    hidden = w_gate.shape[1]
    anywhere = pl.BlockSpec(memory_space=pl.ANY)
    vmem = pl.BlockSpec(memory_space=pltpu.VMEM)

    def buffer(*shape):
        return pltpu.VMEM(shape, jnp.bfloat16)

    return pl.pallas_call(
        functools.partial(expert_kernel, groups),
        out_shape=jax.ShapeDtypeStruct(slabs.shape, jnp.bfloat16),
        in_specs=[vmem, anywhere, anywhere, anywhere],
        out_specs=vmem,
        scratch_shapes=[
            buffer(groups, MEMBERS, slots, width),
            buffer(groups, MEMBERS, slots, width),
            buffer(groups, 2, slots, width),
            buffer(groups, slots, width),
            buffer(groups, slots, width),
            buffer(groups, slots, width),
            buffer(hidden, width),
            buffer(hidden, width),
            buffer(hidden, width),
            pltpu.SemaphoreType.DMA((3,)),
            pltpu.SemaphoreType.DMA((8, groups)),
            pltpu.SemaphoreType.DMA((8, groups)),
        ],
        compiler_params=pltpu.CompilerParams(
            collective_id=0, has_side_effects=True, vmem_limit_bytes=56 * 1024 * 1024
        ),
    )(slabs, w_gate, w_up, w_down)


def attention_kernel(
    levels,
    wo_ref,
    query_ref,
    keys_ref,
    values_ref,
    hidden_ref,
    gain_ref,
    attended_ref,
    stream_ref,
    normed_ref,
    wo,
    key_window,
    value_window,
    mixed,
    total,
    kv_send,
    kv_recv,
    send_sem,
    recv_sem,
):
    count = levels * 8
    me = lax.axis_index("ctx")
    level = me // 8
    row = (me // 4) % 2
    column = (me // 2) % 2
    core = me % 2
    sibling = me + 1 - 2 * core

    def place(at, first, second):
        down = first * (1 - core) + second * core
        over = first * core + second * (1 - core)
        return (
            (at * 2 + row + down * (1 - 2 * row)) * 4
            + (column + over * (1 - 2 * column)) * 2
            + core
        )

    def send(slot, kind, index, device):
        return pltpu.make_async_remote_copy(
            src_ref=wo.at[slot],
            dst_ref=wo.at[slot],
            send_sem=send_sem.at[kind, index],
            recv_sem=recv_sem.at[slot],
            device_id={"ctx": device},
            device_id_type=pl.DeviceIdType.MESH,
        )

    across, beyond = place(level, 1, 0), place(level, 0, 1)

    def along(at):
        return send(me, 0, at, place(at, 0, 0))

    def to_first(at):
        return send(place(at, 0, 0), 1, at, across)

    def to_second(at, first):
        return send(place(at, first, 0), 2 + first, at, beyond)

    def to_sibling(at, first, second):
        return send(place(at, first, second), 4 + 2 * first + second, at, sibling)

    def arrived(slot):
        send(slot, 0, 0, sibling).wait_recv()

    def kv_copy(part, distance):
        source = (keys_ref, values_ref)[part]
        target = (key_window, value_window)[part]
        return pltpu.make_async_remote_copy(
            src_ref=source,
            dst_ref=target.at[3 - distance],
            send_sem=kv_send.at[part, distance - 1],
            recv_sem=kv_recv.at[part, distance - 1],
            device_id={"ctx": lax.rem(me + distance, count)},
            device_id_type=pl.DeviceIdType.MESH,
        )

    barrier = pltpu.get_barrier_semaphore()

    def greet(device):
        pl.semaphore_signal(
            barrier, inc=1, device_id={"ctx": device}, device_id_type=pl.DeviceIdType.MESH
        )

    @pl.loop(1, levels)
    def _(o):
        greet(place(lax.rem(level + o, levels), 0, 0))

    for device in (sibling, across, beyond):
        greet(device)
    for distance in (1, 2, 3):
        greet(lax.rem(me + distance, count))
        greet(lax.rem(me - distance + count, count))
    wo[me] = wo_ref[...]
    key_window[3] = keys_ref[...]
    value_window[3] = values_ref[...]
    pl.semaphore_wait(barrier, levels - 1 + 9)

    for distance in (1, 2, 3):
        for part in (0, 1):
            kv_copy(part, distance).start()

    @pl.loop(1, levels)
    def _(o):
        along(lax.rem(level + o, levels)).start()

    total[...] = jnp.zeros_like(total)
    tok_rows = query_ref.shape[0]
    window = 4 * tok_rows
    width = total.shape[1]
    block_rows = wo.shape[1]
    group_size = HEADS // KV_HEADS
    chunk = group_size * HEAD_DIM

    def attend(g):
        pair = pl.ds(pl.multiple_of(g // 2 * 2 * HEAD_DIM, 2 * HEAD_DIM), 2 * HEAD_DIM)
        even = g % 2 == 0
        key_pair = key_window[:, :, pair].reshape(window, 2 * HEAD_DIM)
        value_pair = value_window[:, :, pair].reshape(window, 2 * HEAD_DIM)
        head_keys = jnp.where(even, key_pair[:, :HEAD_DIM], key_pair[:, HEAD_DIM:])
        head_values = jnp.where(even, value_pair[:, :HEAD_DIM], value_pair[:, HEAD_DIM:])
        at = pl.ds(pl.multiple_of(g * chunk, chunk), chunk)
        queries = query_ref[:, at]
        query_pos = lax.broadcasted_iota(jnp.int32, (tok_rows, window), 0)
        key_pos = lax.broadcasted_iota(jnp.int32, (tok_rows, window), 1) - 3 * tok_rows
        allowed = (key_pos <= query_pos) & (key_pos + me * tok_rows >= 0)
        for h in range(group_size):
            lanes = slice(h * HEAD_DIM, (h + 1) * HEAD_DIM)
            scores = lax.dot_general(
                queries[:, lanes],
                head_keys,
                (((1,), (1,)), ((), ())),
                preferred_element_type=jnp.float32,
            ) * HEAD_DIM ** (-0.5)
            scores = jnp.where(allowed, scores, -1e30)
            top_score = jnp.max(scores, axis=-1, keepdims=True)
            weights = jnp.where(allowed, jnp.exp(scores - top_score), 0.0)
            probs = weights * (1.0 / jnp.sum(weights, axis=-1, keepdims=True))
            mixed[:, lanes] = jnp.dot(
                probs.astype(jnp.bfloat16), head_values, preferred_element_type=jnp.float32
            ).astype(jnp.bfloat16)
        attended_ref[:, at] = mixed[...]

    def level_at(step):
        return lax.rem(level - step + levels, levels)

    @pl.loop(0, levels + 3)
    def _(t):
        @pl.when(t < levels)
        def _():
            at = level_at(t)

            @pl.when(t > 0)
            def _():
                arrived(place(at, 0, 0))

            to_first(at).start()
            to_second(at, 0).start()
            to_sibling(at, 0, 0).start()

        @pl.when(t == 0)
        def _():
            for distance in (1, 2, 3):
                for part in (0, 1):
                    kv_copy(part, distance).wait_recv()

        @pl.when((t >= 1) & (t < levels + 1))
        def _():
            at = level_at(t - 1)
            arrived(place(at, 1, 0))
            to_second(at, 1).start()
            to_sibling(at, 1, 0).start()

        @pl.when(t < KV_HEADS)
        def _():
            attend(t)

        @pl.when((t >= 2) & (t < levels + 2))
        def _():
            at = level_at(t - 2)
            for first in (0, 1):
                arrived(place(at, first, 1))
                to_sibling(at, first, 1).start()

        @pl.when(t >= 3)
        def _():
            at = level_at(t - 3)
            for group in (at * 2, at * 2 + 1):
                for member in (0, 2):
                    arrived(group * 4 + member + 1 - core)
                depth = 4 * block_rows
                rows = wo[pl.ds(group * 4, 4)].reshape(depth, width)
                heads = attended_ref[:, pl.ds(pl.multiple_of(group * depth, depth), depth)]
                for start in range(0, width, 768):
                    span = slice(start, min(start + 768, width))
                    total[:, span] += jnp.dot(
                        heads, rows[:, span], preferred_element_type=jnp.float32
                    )

    stream = (hidden_ref[...].astype(jnp.float32) + total[...]).astype(jnp.bfloat16)
    stream_ref[...] = stream
    features = stream.astype(jnp.float32)
    normed_ref[...] = (
        features
        * lax.rsqrt(jnp.mean(features * features, axis=-1, keepdims=True) + 1e-05)
        * gain_ref[...].astype(jnp.float32)
    ).astype(jnp.bfloat16)

    @pl.loop(0, levels)
    def _(at):
        to_first(at).wait_send()
        for first in (0, 1):
            to_second(at, first).wait_send()
            for second in (0, 1):
                to_sibling(at, first, second).wait_send()

    @pl.loop(1, levels)
    def _(o):
        along(lax.rem(level + o, levels)).wait_send()

    for distance in (1, 2, 3):
        for part in (0, 1):
            kv_copy(part, distance).wait_send()


def attention_call(o_proj, query, keys, values, hidden_states, norm_gain):
    devices = lax.axis_size("ctx")
    levels = devices // 8
    block_rows, width = o_proj.shape
    tok_rows = query.shape[0]

    def buffer(*shape):
        return pltpu.VMEM(shape, jnp.bfloat16)

    return pl.pallas_call(
        functools.partial(attention_kernel, levels),
        out_shape=[
            jax.ShapeDtypeStruct(query.shape, jnp.bfloat16),
            jax.ShapeDtypeStruct(hidden_states.shape, jnp.bfloat16),
            jax.ShapeDtypeStruct(hidden_states.shape, jnp.bfloat16),
        ],
        in_specs=[pl.BlockSpec(memory_space=pltpu.VMEM)] * 6,
        out_specs=[pl.BlockSpec(memory_space=pltpu.VMEM)] * 3,
        scratch_shapes=[
            buffer(devices, block_rows, width),
            buffer(4, tok_rows, keys.shape[1]),
            buffer(4, tok_rows, keys.shape[1]),
            buffer(tok_rows, HEADS // KV_HEADS * HEAD_DIM),
            pltpu.VMEM((tok_rows, width), jnp.float32),
            pltpu.SemaphoreType.DMA((2, 3)),
            pltpu.SemaphoreType.DMA((2, 3)),
            pltpu.SemaphoreType.DMA((8, levels)),
            pltpu.SemaphoreType.DMA((devices,)),
        ],
        compiler_params=pltpu.CompilerParams(
            collective_id=1, has_side_effects=True, vmem_limit_bytes=48 * 1024 * 1024
        ),
    )(o_proj, query, keys, values, hidden_states, norm_gain.reshape(1, -1))


def local(
    hidden_states,
    o_proj,
    norm_gain,
    router_weight,
    routes,
    w_gate,
    w_up,
    w_down,
    query,
    keys,
    values,
):
    tok_rows = hidden_states.shape[0]
    model_width = hidden_states.shape[1]
    per_token = routes.shape[1]
    experts = router_weight.shape[1]
    devices = lax.axis_size("ctx")
    shard_count = devices // experts
    capacity = min(tok_rows, (tok_rows * per_token // experts // shard_count + 1) * shard_count)
    slots = -(-capacity // 8) * 8
    attended, stream, normed = attention_call(
        o_proj, query, keys, values, hidden_states, norm_gain
    )
    features = stream.astype(jnp.float32)
    logits = jnp.dot(normed, router_weight, preferred_element_type=jnp.float32)
    choices = jnp.arange(experts, dtype=jnp.int32)
    named = jnp.any(routes[:, :, None] == choices, axis=1)
    top_logit = jnp.max(jnp.where(named, logits, -jnp.inf), axis=-1, keepdims=True)
    raw = jnp.where(named, jnp.exp(jnp.where(named, logits - top_logit, 0.0)), 0.0)
    route_weight = raw / jnp.sum(raw, axis=-1, keepdims=True)
    tokens = jnp.arange(tok_rows, dtype=jnp.int32)
    earlier = (tokens[None, :] < tokens[:, None]).astype(jnp.bfloat16)
    rank = jnp.dot(earlier, named.astype(jnp.bfloat16), preferred_element_type=jnp.float32)
    slot_index = jnp.arange(slots, dtype=jnp.int32)
    assign = named[:, :, None] & (rank.astype(jnp.int32)[:, :, None] == slot_index)
    place = assign.astype(jnp.bfloat16).reshape(tok_rows, experts * slots)
    slabs = lax.dot_general(
        place, normed, (((0,), (0,)), ((), ())), preferred_element_type=jnp.float32
    ).astype(jnp.bfloat16).reshape(experts, slots, model_width)
    summed = experts_call(
        slabs, jnp.swapaxes(w_gate, 1, 2), jnp.swapaxes(w_up, 1, 2), w_down
    ).reshape(experts * slots, model_width)
    weights = jnp.where(assign, route_weight[:, :, None], 0.0).reshape(tok_rows, experts * slots)
    upper = weights.astype(jnp.bfloat16)
    lower = (weights - upper.astype(jnp.float32)).astype(jnp.bfloat16)
    both = jnp.dot(
        jnp.concatenate([upper, lower]), summed, preferred_element_type=jnp.float32
    )
    moe_output = (features + both[:tok_rows] + both[tok_rows:]).astype(jnp.bfloat16)
    return (moe_output, attended)


def solution(mesh):
    in_specs = (
        P(("parts", "ctx"), None),
        P("ctx", None),
        P(),
        P(),
        P(("parts", "ctx"), None),
        P("ctx", None, None),
        P("ctx", None, None),
        P("ctx", None, None),
        P(("parts", "ctx"), None),
        P(("parts", "ctx"), None),
        P(("parts", "ctx"), None),
    )
    out_specs = (P(("parts", "ctx"), None), P(("parts", "ctx"), None))
    return jax.shard_map(local, mesh=mesh, in_specs=in_specs, out_specs=out_specs, check_vma=False)
```

```python
import functools

import jax
import jax.numpy as jnp
from jax import lax
from jax.experimental import pallas as pl
from jax.experimental.pallas import tpu as pltpu
from jax.sharding import PartitionSpec as P

HEADS = 32
KV_HEADS = 4
HEAD_DIM = 64


MEMBERS = 4
AHEAD_GATHER = 2
AHEAD_EXPERTS = 2


def xor(a, b, count):
    result, bit = 0, 1
    while bit < count:
        result += (a // bit + b // bit) % 2 * bit
        bit *= 2
    return result


def expert_kernel(
    groups,
    slab_ref,
    gate_hbm,
    up_hbm,
    down_hbm,
    out_ref,
    recv,
    pieces,
    near,
    pair_sum,
    far,
    final,
    gate_ref,
    up_ref,
    down_ref,
    weight_sem,
    send_sem,
    recv_sem,
):
    me = lax.axis_index("ctx")
    group = me // MEMBERS
    j = me % MEMBERS
    j_sib = j + 1 - 2 * (j % 2)
    j_far = (j + 2) % MEMBERS
    j_diag = MEMBERS - 1 - j
    sibling = group * MEMBERS + j_sib
    partner = group * MEMBERS + j_far

    def to(src, dst, kind, here, there, device):
        return pltpu.make_async_remote_copy(
            src_ref=src,
            dst_ref=dst,
            send_sem=send_sem.at[kind, here],
            recv_sem=recv_sem.at[kind, there],
            device_id={"ctx": device},
            device_id_type=pl.DeviceIdType.MESH,
        )

    weight_copies = [
        pltpu.make_async_copy(src, dst, weight_sem.at[i])
        for i, (src, dst) in enumerate(
            ((gate_hbm.at[0], gate_ref), (up_hbm.at[0], up_ref), (down_hbm.at[0], down_ref))
        )
    ]
    for copy in weight_copies:
        copy.start()

    barrier = pltpu.get_barrier_semaphore()

    def greet(device):
        pl.semaphore_signal(
            barrier, inc=1, device_id={"ctx": device}, device_id_type=pl.DeviceIdType.MESH
        )

    @pl.loop(1, groups)
    def _(o):
        greet(lax.rem(group + o, groups) * MEMBERS + j)

    greet(sibling)
    greet(partner)
    pl.semaphore_wait(barrier, groups + 1)

    def scatter(target):
        return to(
            slab_ref.at[target], recv.at[group, j], 0, target, group, target * MEMBERS + j
        )

    def scattered(s):
        return to(slab_ref.at[s], recv.at[s, j], 0, s, s, sibling)

    def share_sibling(s):
        return to(recv.at[s, j], recv.at[s, j], 1, s, s, sibling)

    def share_partner(s):
        return to(recv.at[s, j], recv.at[s, j], 2, s, s, partner)

    def share_diag(s):
        return to(recv.at[s, j_far], recv.at[s, j_far], 3, s, s, sibling)

    def piece_near(s):
        return to(pieces.at[s, j_sib], near.at[s, 0], 4, s, s, sibling)

    def piece_diag(s):
        return to(pieces.at[s, j_diag], near.at[s, 1], 5, s, s, sibling)

    def piece_far(s):
        return to(pair_sum.at[s], far.at[s], 6, s, s, partner)

    def give_back(s):
        return to(final.at[s], out_ref.at[group], 7, s, group, s * MEMBERS + j)

    def given_back(s):
        return to(final.at[s], out_ref.at[s], 7, s, s, s * MEMBERS + j)

    def source(step):
        return xor(group, step, groups)

    @pl.loop(1, min(AHEAD_EXPERTS + 1, groups))
    def _(o):
        scatter(source(o)).start()

    recv[group, j] = slab_ref[group]

    rows, width = recv.shape[2], recv.shape[3]

    @pl.loop(0, groups + 4)
    def _(t):
        @pl.when(t < groups)
        def _():
            s = source(t)

            @pl.when(t > 0)
            def _():
                scattered(s).wait_recv()

            share_partner(s).start()

            @pl.when((t > 0) & (t + AHEAD_EXPERTS < groups))
            def _():
                scatter(source(t + AHEAD_EXPERTS)).start()

            share_sibling(s).start()

        @pl.when((t >= 1) & (t < groups + 1))
        def _():
            s = source(t - 1)
            share_partner(s).wait_recv()
            share_diag(s).start()

        @pl.when((t >= 4) & (t < groups + 4))
        def _():
            s = source(t - 4)
            piece_far(s).wait_recv()
            total = (
                pieces[s, j].astype(jnp.float32)
                + near[s, 0].astype(jnp.float32)
                + far[s].astype(jnp.float32)
            ).astype(jnp.bfloat16)

            @pl.when(t == 4)
            def _():
                out_ref[group] = total

            @pl.when(t > 4)
            def _():
                final[s] = total
                give_back(s).start()

        @pl.when((t >= 3) & (t < groups + 3))
        def _():
            s = source(t - 3)
            piece_near(s).wait_recv()
            piece_diag(s).wait_recv()
            pair_sum[s] = (
                pieces[s, j_far].astype(jnp.float32) + near[s, 1].astype(jnp.float32)
            ).astype(jnp.bfloat16)
            piece_far(s).start()

        @pl.when((t >= 2) & (t < groups + 2))
        def _():
            s = source(t - 2)

            @pl.when(t == 2)
            def _():
                for copy in weight_copies:
                    copy.wait()

            share_sibling(s).wait_recv()
            share_diag(s).wait_recv()
            block = recv[s].reshape(MEMBERS * rows, width)
            across = (((1,), (1,)), ((), ()))
            gate = lax.dot_general(
                block, gate_ref[...], across, preferred_element_type=jnp.float32
            )
            up = lax.dot_general(block, up_ref[...], across, preferred_element_type=jnp.float32)
            activated = ((up + 1.0) * gate * jax.nn.sigmoid(1.702 * gate)).astype(jnp.bfloat16)
            for at in range(0, width, 768):
                span = slice(at, min(at + 768, width))
                piece = jnp.dot(
                    activated, down_ref[:, span], preferred_element_type=jnp.float32
                ).astype(jnp.bfloat16)
                pieces[s, :, :, span] = piece.reshape(MEMBERS, rows, span.stop - span.start)
            piece_near(s).start()
            piece_diag(s).start()

    @pl.loop(0, groups)
    def _(s):
        share_sibling(s).wait_send()
        share_partner(s).wait_send()
        share_diag(s).wait_send()
        piece_near(s).wait_send()
        piece_diag(s).wait_send()
        piece_far(s).wait_send()

    @pl.loop(1, groups)
    def _(o):
        s = source(o)
        scattered(s).wait_send()
        given_back(s).wait_send()
        given_back(s).wait_recv()


def experts_call(slabs, w_gate, w_up, w_down):
    groups, slots, width = slabs.shape
    hidden = w_gate.shape[1]
    anywhere = pl.BlockSpec(memory_space=pl.ANY)
    vmem = pl.BlockSpec(memory_space=pltpu.VMEM)

    def buffer(*shape):
        return pltpu.VMEM(shape, jnp.bfloat16)

    return pl.pallas_call(
        functools.partial(expert_kernel, groups),
        out_shape=jax.ShapeDtypeStruct(slabs.shape, jnp.bfloat16),
        in_specs=[vmem, anywhere, anywhere, anywhere],
        out_specs=vmem,
        scratch_shapes=[
            buffer(groups, MEMBERS, slots, width),
            buffer(groups, MEMBERS, slots, width),
            buffer(groups, 2, slots, width),
            buffer(groups, slots, width),
            buffer(groups, slots, width),
            buffer(groups, slots, width),
            buffer(hidden, width),
            buffer(hidden, width),
            buffer(hidden, width),
            pltpu.SemaphoreType.DMA((3,)),
            pltpu.SemaphoreType.DMA((8, groups)),
            pltpu.SemaphoreType.DMA((8, groups)),
        ],
        compiler_params=pltpu.CompilerParams(
            collective_id=0, has_side_effects=True, vmem_limit_bytes=56 * 1024 * 1024
        ),
    )(slabs, w_gate, w_up, w_down)


def attention_kernel(
    levels,
    wo_hbm,
    query_hbm,
    keys_hbm,
    values_hbm,
    hidden_hbm,
    gain_hbm,
    attended_ref,
    stream_ref,
    normed_ref,
    wo,
    key_window,
    value_window,
    mixed,
    total,
    query_ref,
    hidden_ref,
    gain_ref,
    load_sem,
    kv_send,
    kv_recv,
    send_sem,
    recv_sem,
):
    count = levels * 8
    me = lax.axis_index("ctx")
    level = me // 8
    row = (me // 4) % 2
    column = (me // 2) % 2
    core = me % 2
    sibling = me + 1 - 2 * core

    def place(at, first, second):
        down = first * (1 - core) + second * core
        over = first * core + second * (1 - core)
        return (
            (at * 2 + row + down * (1 - 2 * row)) * 4
            + (column + over * (1 - 2 * column)) * 2
            + core
        )

    def send(slot, kind, index, device):
        return pltpu.make_async_remote_copy(
            src_ref=wo.at[slot],
            dst_ref=wo.at[slot],
            send_sem=send_sem.at[kind, index],
            recv_sem=recv_sem.at[slot],
            device_id={"ctx": device},
            device_id_type=pl.DeviceIdType.MESH,
        )

    loads = [
        pltpu.make_async_copy(src, dst, load_sem.at[i])
        for i, (src, dst) in enumerate(
            (
                (wo_hbm, wo.at[me]),
                (keys_hbm, key_window.at[3]),
                (values_hbm, value_window.at[3]),
                (query_hbm, query_ref),
                (hidden_hbm, hidden_ref),
                (gain_hbm, gain_ref),
            )
        )
    ]
    for load in loads:
        load.start()
    across, beyond = place(level, 1, 0), place(level, 0, 1)

    def level_at(step):
        return xor(level, step, levels)

    def along(at):
        return send(me, 0, at, place(at, 0, 0))

    def to_first(at):
        return send(place(at, 0, 0), 1, at, across)

    def to_second(at, first):
        return send(place(at, first, 0), 2 + first, at, beyond)

    def to_sibling(at, first, second):
        return send(place(at, first, second), 4 + 2 * first + second, at, sibling)

    def arrived(slot):
        send(slot, 0, 0, sibling).wait_recv()

    def kv_copy(part, distance):
        target = (key_window, value_window)[part]
        return pltpu.make_async_remote_copy(
            src_ref=target.at[3],
            dst_ref=target.at[3 - distance],
            send_sem=kv_send.at[part, distance - 1],
            recv_sem=kv_recv.at[part, distance - 1],
            device_id={"ctx": lax.rem(me + distance, count)},
            device_id_type=pl.DeviceIdType.MESH,
        )

    barrier = pltpu.get_barrier_semaphore()

    def greet(device):
        pl.semaphore_signal(
            barrier, inc=1, device_id={"ctx": device}, device_id_type=pl.DeviceIdType.MESH
        )

    @pl.loop(1, levels)
    def _(o):
        greet(place(lax.rem(level + o, levels), 0, 0))

    for device in (sibling, across, beyond):
        greet(device)
    for distance in (1, 2, 3):
        greet(lax.rem(me + distance, count))
        greet(lax.rem(me - distance + count, count))
    for load in loads[:3]:
        load.wait()
    pl.semaphore_wait(barrier, levels - 1 + 9)

    for distance in (1, 2, 3):
        for part in (0, 1):
            kv_copy(part, distance).start()

    @pl.loop(1, min(AHEAD_GATHER + 1, levels))
    def _(o):
        along(level_at(o)).start()

    total[...] = jnp.zeros_like(total)
    for load in loads[3:]:
        load.wait()
    tok_rows = query_ref.shape[0]
    window = 4 * tok_rows
    width = total.shape[1]
    block_rows = wo.shape[1]
    group_size = HEADS // KV_HEADS
    chunk = group_size * HEAD_DIM

    def attend(g):
        pair = pl.ds(pl.multiple_of(g // 2 * 2 * HEAD_DIM, 2 * HEAD_DIM), 2 * HEAD_DIM)
        even = g % 2 == 0
        key_pair = key_window[:, :, pair].reshape(window, 2 * HEAD_DIM)
        value_pair = value_window[:, :, pair].reshape(window, 2 * HEAD_DIM)
        head_keys = jnp.where(even, key_pair[:, :HEAD_DIM], key_pair[:, HEAD_DIM:])
        head_values = jnp.where(even, value_pair[:, :HEAD_DIM], value_pair[:, HEAD_DIM:])
        at = pl.ds(pl.multiple_of(g * chunk, chunk), chunk)
        queries = query_ref[:, at]
        query_pos = lax.broadcasted_iota(jnp.int32, (tok_rows, window), 0)
        key_pos = lax.broadcasted_iota(jnp.int32, (tok_rows, window), 1) - 3 * tok_rows
        allowed = (key_pos <= query_pos) & (key_pos + me * tok_rows >= 0)
        for h in range(group_size):
            lanes = slice(h * HEAD_DIM, (h + 1) * HEAD_DIM)
            scores = lax.dot_general(
                queries[:, lanes],
                head_keys,
                (((1,), (1,)), ((), ())),
                preferred_element_type=jnp.float32,
            ) * HEAD_DIM ** (-0.5)
            scores = jnp.where(allowed, scores, -1e30)
            top_score = jnp.max(scores, axis=-1, keepdims=True)
            weights = jnp.where(allowed, jnp.exp(scores - top_score), 0.0)
            probs = weights * (1.0 / jnp.sum(weights, axis=-1, keepdims=True))
            mixed[:, lanes] = jnp.dot(
                probs.astype(jnp.bfloat16), head_values, preferred_element_type=jnp.float32
            ).astype(jnp.bfloat16)
        attended_ref[:, at] = mixed[...]

    @pl.loop(0, levels + 3)
    def _(t):
        @pl.when(t < levels)
        def _():
            at = level_at(t)

            @pl.when(t > 0)
            def _():
                arrived(place(at, 0, 0))

            to_first(at).start()
            to_second(at, 0).start()

            @pl.when((t > 0) & (t + AHEAD_GATHER < levels))
            def _():
                along(level_at(t + AHEAD_GATHER)).start()

            to_sibling(at, 0, 0).start()

        @pl.when(t == 0)
        def _():
            for distance in (1, 2, 3):
                for part in (0, 1):
                    kv_copy(part, distance).wait_recv()

        @pl.when((t >= 1) & (t < levels + 1))
        def _():
            at = level_at(t - 1)
            arrived(place(at, 1, 0))
            to_second(at, 1).start()
            to_sibling(at, 1, 0).start()

        @pl.when(t < KV_HEADS)
        def _():
            attend(t)

        @pl.when((t >= 2) & (t < levels + 2))
        def _():
            at = level_at(t - 2)
            for first in (0, 1):
                arrived(place(at, first, 1))
                to_sibling(at, first, 1).start()

        @pl.when(t >= 3)
        def _():
            at = level_at(t - 3)
            for group in (at * 2, at * 2 + 1):
                for member in (0, 2):
                    arrived(group * 4 + member + 1 - core)
                depth = 4 * block_rows
                rows = wo[pl.ds(group * 4, 4)].reshape(depth, width)
                heads = attended_ref[:, pl.ds(pl.multiple_of(group * depth, depth), depth)]
                for start in range(0, width, 768):
                    span = slice(start, min(start + 768, width))
                    total[:, span] += jnp.dot(
                        heads, rows[:, span], preferred_element_type=jnp.float32
                    )

    stream = (hidden_ref[...].astype(jnp.float32) + total[...]).astype(jnp.bfloat16)
    stream_ref[...] = stream
    features = stream.astype(jnp.float32)
    normed_ref[...] = (
        features
        * lax.rsqrt(jnp.mean(features * features, axis=-1, keepdims=True) + 1e-05)
        * gain_ref[...].astype(jnp.float32)
    ).astype(jnp.bfloat16)

    @pl.loop(0, levels)
    def _(at):
        to_first(at).wait_send()
        for first in (0, 1):
            to_second(at, first).wait_send()
            for second in (0, 1):
                to_sibling(at, first, second).wait_send()

    @pl.loop(1, levels)
    def _(o):
        along(lax.rem(level + o, levels)).wait_send()

    for distance in (1, 2, 3):
        for part in (0, 1):
            kv_copy(part, distance).wait_send()


def attention_call(o_proj, query, keys, values, hidden_states, norm_gain):
    devices = lax.axis_size("ctx")
    levels = devices // 8
    block_rows, width = o_proj.shape
    tok_rows = query.shape[0]

    def buffer(*shape):
        return pltpu.VMEM(shape, jnp.bfloat16)

    return pl.pallas_call(
        functools.partial(attention_kernel, levels),
        out_shape=[
            jax.ShapeDtypeStruct(query.shape, jnp.bfloat16),
            jax.ShapeDtypeStruct(hidden_states.shape, jnp.bfloat16),
            jax.ShapeDtypeStruct(hidden_states.shape, jnp.bfloat16),
        ],
        in_specs=[pl.BlockSpec(memory_space=pl.ANY)] * 6,
        out_specs=[pl.BlockSpec(memory_space=pltpu.VMEM)] * 3,
        scratch_shapes=[
            buffer(devices, block_rows, width),
            buffer(4, tok_rows, keys.shape[1]),
            buffer(4, tok_rows, keys.shape[1]),
            buffer(tok_rows, HEADS // KV_HEADS * HEAD_DIM),
            pltpu.VMEM((tok_rows, width), jnp.float32),
            buffer(*query.shape),
            buffer(*hidden_states.shape),
            buffer(1, width),
            pltpu.SemaphoreType.DMA((6,)),
            pltpu.SemaphoreType.DMA((2, 3)),
            pltpu.SemaphoreType.DMA((2, 3)),
            pltpu.SemaphoreType.DMA((8, levels)),
            pltpu.SemaphoreType.DMA((devices,)),
        ],
        compiler_params=pltpu.CompilerParams(
            collective_id=1, has_side_effects=True, vmem_limit_bytes=56 * 1024 * 1024
        ),
    )(o_proj, query, keys, values, hidden_states, norm_gain.reshape(1, -1))


def local(
    hidden_states,
    o_proj,
    norm_gain,
    router_weight,
    routes,
    w_gate,
    w_up,
    w_down,
    query,
    keys,
    values,
):
    tok_rows = hidden_states.shape[0]
    model_width = hidden_states.shape[1]
    per_token = routes.shape[1]
    experts = router_weight.shape[1]
    devices = lax.axis_size("ctx")
    shard_count = devices // experts
    capacity = min(tok_rows, (tok_rows * per_token // experts // shard_count + 1) * shard_count)
    slots = -(-capacity // 8) * 8
    attended, stream, normed = attention_call(
        o_proj, query, keys, values, hidden_states, norm_gain
    )
    features = stream.astype(jnp.float32)
    logits = jnp.dot(normed, router_weight, preferred_element_type=jnp.float32)
    choices = jnp.arange(experts, dtype=jnp.int32)
    named = jnp.any(routes[:, :, None] == choices, axis=1)
    top_logit = jnp.max(jnp.where(named, logits, -jnp.inf), axis=-1, keepdims=True)
    raw = jnp.where(named, jnp.exp(jnp.where(named, logits - top_logit, 0.0)), 0.0)
    route_weight = raw / jnp.sum(raw, axis=-1, keepdims=True)
    tokens = jnp.arange(tok_rows, dtype=jnp.int32)
    earlier = (tokens[None, :] < tokens[:, None]).astype(jnp.bfloat16)
    rank = jnp.dot(earlier, named.astype(jnp.bfloat16), preferred_element_type=jnp.float32)
    slot_index = jnp.arange(slots, dtype=jnp.int32)
    assign = named[:, :, None] & (rank.astype(jnp.int32)[:, :, None] == slot_index)
    place = assign.astype(jnp.bfloat16).reshape(tok_rows, experts * slots)
    slabs = lax.dot_general(
        place, normed, (((0,), (0,)), ((), ())), preferred_element_type=jnp.float32
    ).astype(jnp.bfloat16).reshape(experts, slots, model_width)
    summed = experts_call(
        slabs, jnp.swapaxes(w_gate, 1, 2), jnp.swapaxes(w_up, 1, 2), w_down
    ).reshape(experts * slots, model_width)
    weights = jnp.where(assign, route_weight[:, :, None], 0.0).reshape(tok_rows, experts * slots)
    upper = weights.astype(jnp.bfloat16)
    lower = (weights - upper.astype(jnp.float32)).astype(jnp.bfloat16)
    both = jnp.dot(
        jnp.concatenate([upper, lower]), summed, preferred_element_type=jnp.float32
    )
    moe_output = (features + both[:tok_rows] + both[tok_rows:]).astype(jnp.bfloat16)
    return (moe_output, attended)


def solution(mesh):
    in_specs = (
        P(("parts", "ctx"), None),
        P("ctx", None),
        P(),
        P(),
        P(("parts", "ctx"), None),
        P("ctx", None, None),
        P("ctx", None, None),
        P("ctx", None, None),
        P(("parts", "ctx"), None),
        P(("parts", "ctx"), None),
        P(("parts", "ctx"), None),
    )
    out_specs = (P(("parts", "ctx"), None), P(("parts", "ctx"), None))
    return jax.shard_map(local, mesh=mesh, in_specs=in_specs, out_specs=out_specs, check_vma=False)
```

```python
import functools

import jax
import jax.numpy as jnp
from jax import lax
from jax.experimental import pallas as pl
from jax.experimental.pallas import tpu as pltpu
from jax.sharding import PartitionSpec as P

HEADS = 32
KV_HEADS = 4
HEAD_DIM = 64


MEMBERS = 4
AHEAD_GATHER = 2
AHEAD_EXPERTS = 2


def xor(a, b, count):
    result, bit = 0, 1
    while bit < count:
        result += (a // bit + b // bit) % 2 * bit
        bit *= 2
    return result


def expert_kernel(
    groups,
    normed_ref,
    place_ref,
    gate_hbm,
    up_hbm,
    down_hbm,
    out_ref,
    recv,
    pieces,
    near,
    pair_sum,
    far,
    final,
    gate_ref,
    up_ref,
    down_ref,
    dense,
    placed,
    cross,
    weight_sem,
    send_sem,
    recv_sem,
):
    me = lax.axis_index("ctx")
    group = me // MEMBERS
    j = me % MEMBERS
    j_sib = j + 1 - 2 * (j % 2)
    j_far = (j + 2) % MEMBERS
    j_diag = MEMBERS - 1 - j
    sibling = group * MEMBERS + j_sib
    partner = group * MEMBERS + j_far

    def to(src, dst, kind, here, there, device):
        return pltpu.make_async_remote_copy(
            src_ref=src,
            dst_ref=dst,
            send_sem=send_sem.at[kind, here],
            recv_sem=recv_sem.at[kind, there],
            device_id={"ctx": device},
            device_id_type=pl.DeviceIdType.MESH,
        )

    weight_copies = [
        pltpu.make_async_copy(src, dst, weight_sem.at[i])
        for i, (src, dst) in enumerate(
            ((gate_hbm.at[0], gate_ref), (up_hbm.at[0], up_ref), (down_hbm.at[0], down_ref))
        )
    ]
    for copy in weight_copies:
        copy.start()

    barrier = pltpu.get_barrier_semaphore()

    def greet(device):
        pl.semaphore_signal(
            barrier, inc=1, device_id={"ctx": device}, device_id_type=pl.DeviceIdType.MESH
        )

    @pl.loop(1, groups)
    def _(o):
        greet(lax.rem(group + o, groups) * MEMBERS + j)

    greet(sibling)
    greet(partner)
    pl.semaphore_wait(barrier, groups + 1)

    levels = groups // 2
    level, row = group // 2, group % 2

    def whole(kind, src, dst, at, there):
        return to(src, dst, kind, at, there, (at * 2 + row) * MEMBERS + j)

    def send_block(at):
        return (
            whole(0, normed_ref, dense.at[level], at, level),
            whole(8, place_ref.at[pl.ds(at * 2, 2)], placed.at[level], at, level),
        )

    def block_arrived(at):
        return (
            whole(0, normed_ref, dense.at[at], at, at),
            whole(8, place_ref.at[pl.ds(at * 2, 2)], placed.at[at], at, at),
        )

    def send_cross(at):
        return to(
            cross.at[at],
            recv.at[at * 2 + row, j],
            9,
            at,
            at,
            (level * 2 + 1 - row) * MEMBERS + j,
        )

    def level_at(step):
        return xor(level, step, levels)

    def share_sibling(s):
        return to(recv.at[s, j], recv.at[s, j], 1, s, s, sibling)

    def share_partner(s):
        return to(recv.at[s, j], recv.at[s, j], 2, s, s, partner)

    def share_diag(s):
        return to(recv.at[s, j_far], recv.at[s, j_far], 3, s, s, sibling)

    def piece_near(s):
        return to(pieces.at[s, j_sib], near.at[s, 0], 4, s, s, sibling)

    def piece_diag(s):
        return to(pieces.at[s, j_diag], near.at[s, 1], 5, s, s, sibling)

    def piece_far(s):
        return to(pair_sum.at[s], far.at[s], 6, s, s, partner)

    def give_back(s):
        return to(final.at[s], out_ref.at[group], 7, s, group, s * MEMBERS + j)

    def given_back(s):
        return to(final.at[s], out_ref.at[s], 7, s, s, s * MEMBERS + j)

    def source(step):
        return xor(group, step, groups)

    @pl.loop(1, min(AHEAD_EXPERTS + 1, levels))
    def _(o):
        for copy in send_block(level_at(o)):
            copy.start()

    dense[level] = normed_ref[...]
    placed[level] = place_ref[pl.ds(level * 2, 2)]

    rows, width = recv.shape[2], recv.shape[3]

    @pl.loop(0, groups + 4)
    def _(t):
        @pl.when(t < groups)
        def _():
            s = source(t)

            at = s // 2

            @pl.when(t % 2 == 0)
            def _():
                @pl.when(t > 0)
                def _():
                    for copy in block_arrived(at):
                        copy.wait_recv()

                @pl.when((t > 0) & (t // 2 + AHEAD_EXPERTS < levels))
                def _():
                    for copy in send_block(level_at(t // 2 + AHEAD_EXPERTS)):
                        copy.start()

                cross[at] = jnp.dot(
                    placed[at, 1 - row], dense[at], preferred_element_type=jnp.float32
                ).astype(jnp.bfloat16)
                send_cross(at).start()
                recv[s, j] = jnp.dot(
                    placed[at, row], dense[at], preferred_element_type=jnp.float32
                ).astype(jnp.bfloat16)

            @pl.when(t % 2 == 1)
            def _():
                send_cross(at).wait_recv()

            share_partner(s).start()
            share_sibling(s).start()

        @pl.when((t >= 1) & (t < groups + 1))
        def _():
            s = source(t - 1)
            share_partner(s).wait_recv()
            share_diag(s).start()

        @pl.when((t >= 4) & (t < groups + 4))
        def _():
            s = source(t - 4)
            piece_far(s).wait_recv()
            total = (
                pieces[s, j].astype(jnp.float32)
                + near[s, 0].astype(jnp.float32)
                + far[s].astype(jnp.float32)
            ).astype(jnp.bfloat16)

            @pl.when(t == 4)
            def _():
                out_ref[group] = total

            @pl.when(t > 4)
            def _():
                final[s] = total
                give_back(s).start()

        @pl.when((t >= 3) & (t < groups + 3))
        def _():
            s = source(t - 3)
            piece_near(s).wait_recv()
            piece_diag(s).wait_recv()
            pair_sum[s] = (
                pieces[s, j_far].astype(jnp.float32) + near[s, 1].astype(jnp.float32)
            ).astype(jnp.bfloat16)
            piece_far(s).start()

        @pl.when((t >= 2) & (t < groups + 2))
        def _():
            s = source(t - 2)

            @pl.when(t == 2)
            def _():
                for copy in weight_copies:
                    copy.wait()

            share_sibling(s).wait_recv()
            share_diag(s).wait_recv()
            block = recv[s].reshape(MEMBERS * rows, width)
            across = (((1,), (1,)), ((), ()))
            gate = lax.dot_general(
                block, gate_ref[...], across, preferred_element_type=jnp.float32
            )
            up = lax.dot_general(block, up_ref[...], across, preferred_element_type=jnp.float32)
            activated = ((up + 1.0) * gate * jax.nn.sigmoid(1.702 * gate)).astype(jnp.bfloat16)
            for at in range(0, width, 768):
                span = slice(at, min(at + 768, width))
                piece = jnp.dot(
                    activated, down_ref[:, span], preferred_element_type=jnp.float32
                ).astype(jnp.bfloat16)
                pieces[s, :, :, span] = piece.reshape(MEMBERS, rows, span.stop - span.start)
            piece_near(s).start()
            piece_diag(s).start()

    @pl.loop(0, groups)
    def _(s):
        share_sibling(s).wait_send()
        share_partner(s).wait_send()
        share_diag(s).wait_send()
        piece_near(s).wait_send()
        piece_diag(s).wait_send()
        piece_far(s).wait_send()

    @pl.loop(0, levels)
    def _(at):
        send_cross(at).wait_send()

    @pl.loop(1, levels)
    def _(o):
        for copy in send_block(level_at(o)):
            copy.wait_send()

    @pl.loop(1, groups)
    def _(o):
        s = source(o)
        given_back(s).wait_send()
        given_back(s).wait_recv()


def experts_call(normed, place, w_gate, w_up, w_down):
    groups, slots, tok_rows = place.shape
    width = normed.shape[1]
    hidden = w_gate.shape[1]
    anywhere = pl.BlockSpec(memory_space=pl.ANY)
    vmem = pl.BlockSpec(memory_space=pltpu.VMEM)

    def buffer(*shape):
        return pltpu.VMEM(shape, jnp.bfloat16)

    return pl.pallas_call(
        functools.partial(expert_kernel, groups),
        out_shape=jax.ShapeDtypeStruct((groups, slots, width), jnp.bfloat16),
        in_specs=[vmem, vmem, anywhere, anywhere, anywhere],
        out_specs=vmem,
        scratch_shapes=[
            buffer(groups, MEMBERS, slots, width),
            buffer(groups, MEMBERS, slots, width),
            buffer(groups, 2, slots, width),
            buffer(groups, slots, width),
            buffer(groups, slots, width),
            buffer(groups, slots, width),
            buffer(hidden, width),
            buffer(hidden, width),
            buffer(hidden, width),
            buffer(groups // 2, tok_rows, width),
            buffer(groups // 2, 2, slots, tok_rows),
            buffer(groups // 2, slots, width),
            pltpu.SemaphoreType.DMA((3,)),
            pltpu.SemaphoreType.DMA((10, groups)),
            pltpu.SemaphoreType.DMA((10, groups)),
        ],
        compiler_params=pltpu.CompilerParams(
            collective_id=0, has_side_effects=True, vmem_limit_bytes=56 * 1024 * 1024
        ),
    )(normed, place, w_gate, w_up, w_down)


def attention_kernel(
    levels,
    wo_hbm,
    query_hbm,
    keys_hbm,
    values_hbm,
    hidden_hbm,
    gain_hbm,
    attended_ref,
    stream_ref,
    normed_ref,
    wo,
    key_window,
    value_window,
    mixed,
    total,
    query_ref,
    hidden_ref,
    gain_ref,
    load_sem,
    kv_send,
    kv_recv,
    send_sem,
    recv_sem,
):
    count = levels * 8
    me = lax.axis_index("ctx")
    level = me // 8
    row = (me // 4) % 2
    column = (me // 2) % 2
    core = me % 2
    sibling = me + 1 - 2 * core

    def place(at, first, second):
        down = first * (1 - core) + second * core
        over = first * core + second * (1 - core)
        return (
            (at * 2 + row + down * (1 - 2 * row)) * 4
            + (column + over * (1 - 2 * column)) * 2
            + core
        )

    def send(slot, kind, index, device):
        return pltpu.make_async_remote_copy(
            src_ref=wo.at[slot],
            dst_ref=wo.at[slot],
            send_sem=send_sem.at[kind, index],
            recv_sem=recv_sem.at[slot],
            device_id={"ctx": device},
            device_id_type=pl.DeviceIdType.MESH,
        )

    loads = [
        pltpu.make_async_copy(src, dst, load_sem.at[i])
        for i, (src, dst) in enumerate(
            (
                (wo_hbm, wo.at[me]),
                (keys_hbm, key_window.at[3]),
                (values_hbm, value_window.at[3]),
                (query_hbm, query_ref),
                (hidden_hbm, hidden_ref),
                (gain_hbm, gain_ref),
            )
        )
    ]
    for load in loads:
        load.start()
    across, beyond = place(level, 1, 0), place(level, 0, 1)

    def level_at(step):
        return xor(level, step, levels)

    def along(at):
        return send(me, 0, at, place(at, 0, 0))

    def to_first(at):
        return send(place(at, 0, 0), 1, at, across)

    def to_second(at, first):
        return send(place(at, first, 0), 2 + first, at, beyond)

    def to_sibling(at, first, second):
        return send(place(at, first, second), 4 + 2 * first + second, at, sibling)

    def arrived(slot):
        send(slot, 0, 0, sibling).wait_recv()

    def kv_copy(part, distance):
        target = (key_window, value_window)[part]
        return pltpu.make_async_remote_copy(
            src_ref=target.at[3],
            dst_ref=target.at[3 - distance],
            send_sem=kv_send.at[part, distance - 1],
            recv_sem=kv_recv.at[part, distance - 1],
            device_id={"ctx": lax.rem(me + distance, count)},
            device_id_type=pl.DeviceIdType.MESH,
        )

    barrier = pltpu.get_barrier_semaphore()

    def greet(device):
        pl.semaphore_signal(
            barrier, inc=1, device_id={"ctx": device}, device_id_type=pl.DeviceIdType.MESH
        )

    @pl.loop(1, levels)
    def _(o):
        greet(place(lax.rem(level + o, levels), 0, 0))

    for device in (sibling, across, beyond):
        greet(device)
    for distance in (1, 2, 3):
        greet(lax.rem(me + distance, count))
        greet(lax.rem(me - distance + count, count))
    for load in loads[:3]:
        load.wait()
    pl.semaphore_wait(barrier, levels - 1 + 9)

    for distance in (1, 2, 3):
        for part in (0, 1):
            kv_copy(part, distance).start()

    @pl.loop(1, min(AHEAD_GATHER + 1, levels))
    def _(o):
        along(level_at(o)).start()

    total[...] = jnp.zeros_like(total)
    for load in loads[3:]:
        load.wait()
    tok_rows = query_ref.shape[0]
    window = 4 * tok_rows
    width = total.shape[1]
    block_rows = wo.shape[1]
    group_size = HEADS // KV_HEADS
    chunk = group_size * HEAD_DIM

    def attend(g):
        pair = pl.ds(pl.multiple_of(g // 2 * 2 * HEAD_DIM, 2 * HEAD_DIM), 2 * HEAD_DIM)
        even = g % 2 == 0
        key_pair = key_window[:, :, pair].reshape(window, 2 * HEAD_DIM)
        value_pair = value_window[:, :, pair].reshape(window, 2 * HEAD_DIM)
        head_keys = jnp.where(even, key_pair[:, :HEAD_DIM], key_pair[:, HEAD_DIM:])
        head_values = jnp.where(even, value_pair[:, :HEAD_DIM], value_pair[:, HEAD_DIM:])
        at = pl.ds(pl.multiple_of(g * chunk, chunk), chunk)
        queries = query_ref[:, at]
        query_pos = lax.broadcasted_iota(jnp.int32, (tok_rows, window), 0)
        key_pos = lax.broadcasted_iota(jnp.int32, (tok_rows, window), 1) - 3 * tok_rows
        allowed = (key_pos <= query_pos) & (key_pos + me * tok_rows >= 0)
        for h in range(group_size):
            lanes = slice(h * HEAD_DIM, (h + 1) * HEAD_DIM)
            scores = lax.dot_general(
                queries[:, lanes],
                head_keys,
                (((1,), (1,)), ((), ())),
                preferred_element_type=jnp.float32,
            ) * HEAD_DIM ** (-0.5)
            scores = jnp.where(allowed, scores, -1e30)
            top_score = jnp.max(scores, axis=-1, keepdims=True)
            weights = jnp.where(allowed, jnp.exp(scores - top_score), 0.0)
            probs = weights * (1.0 / jnp.sum(weights, axis=-1, keepdims=True))
            mixed[:, lanes] = jnp.dot(
                probs.astype(jnp.bfloat16), head_values, preferred_element_type=jnp.float32
            ).astype(jnp.bfloat16)
        attended_ref[:, at] = mixed[...]

    @pl.loop(0, levels + 3)
    def _(t):
        @pl.when(t < levels)
        def _():
            at = level_at(t)

            @pl.when(t > 0)
            def _():
                arrived(place(at, 0, 0))

            to_first(at).start()
            to_second(at, 0).start()

            @pl.when((t > 0) & (t + AHEAD_GATHER < levels))
            def _():
                along(level_at(t + AHEAD_GATHER)).start()

            to_sibling(at, 0, 0).start()

        @pl.when(t == 0)
        def _():
            for distance in (1, 2, 3):
                for part in (0, 1):
                    kv_copy(part, distance).wait_recv()

        @pl.when((t >= 1) & (t < levels + 1))
        def _():
            at = level_at(t - 1)
            arrived(place(at, 1, 0))
            to_second(at, 1).start()
            to_sibling(at, 1, 0).start()

        @pl.when(t < KV_HEADS)
        def _():
            attend(t)

        @pl.when((t >= 2) & (t < levels + 2))
        def _():
            at = level_at(t - 2)
            for first in (0, 1):
                arrived(place(at, first, 1))
                to_sibling(at, first, 1).start()

        @pl.when(t >= 3)
        def _():
            at = level_at(t - 3)
            for group in (at * 2, at * 2 + 1):
                for member in (0, 2):
                    arrived(group * 4 + member + 1 - core)
                depth = 4 * block_rows
                rows = wo[pl.ds(group * 4, 4)].reshape(depth, width)
                heads = attended_ref[:, pl.ds(pl.multiple_of(group * depth, depth), depth)]
                for start in range(0, width, 768):
                    span = slice(start, min(start + 768, width))
                    total[:, span] += jnp.dot(
                        heads, rows[:, span], preferred_element_type=jnp.float32
                    )

    stream = (hidden_ref[...].astype(jnp.float32) + total[...]).astype(jnp.bfloat16)
    stream_ref[...] = stream
    features = stream.astype(jnp.float32)
    normed_ref[...] = (
        features
        * lax.rsqrt(jnp.mean(features * features, axis=-1, keepdims=True) + 1e-05)
        * gain_ref[...].astype(jnp.float32)
    ).astype(jnp.bfloat16)

    @pl.loop(0, levels)
    def _(at):
        to_first(at).wait_send()
        for first in (0, 1):
            to_second(at, first).wait_send()
            for second in (0, 1):
                to_sibling(at, first, second).wait_send()

    @pl.loop(1, levels)
    def _(o):
        along(lax.rem(level + o, levels)).wait_send()

    for distance in (1, 2, 3):
        for part in (0, 1):
            kv_copy(part, distance).wait_send()


def attention_call(o_proj, query, keys, values, hidden_states, norm_gain):
    devices = lax.axis_size("ctx")
    levels = devices // 8
    block_rows, width = o_proj.shape
    tok_rows = query.shape[0]

    def buffer(*shape):
        return pltpu.VMEM(shape, jnp.bfloat16)

    return pl.pallas_call(
        functools.partial(attention_kernel, levels),
        out_shape=[
            jax.ShapeDtypeStruct(query.shape, jnp.bfloat16),
            jax.ShapeDtypeStruct(hidden_states.shape, jnp.bfloat16),
            jax.ShapeDtypeStruct(hidden_states.shape, jnp.bfloat16),
        ],
        in_specs=[pl.BlockSpec(memory_space=pl.ANY)] * 6,
        out_specs=[pl.BlockSpec(memory_space=pltpu.VMEM)] * 3,
        scratch_shapes=[
            buffer(devices, block_rows, width),
            buffer(4, tok_rows, keys.shape[1]),
            buffer(4, tok_rows, keys.shape[1]),
            buffer(tok_rows, HEADS // KV_HEADS * HEAD_DIM),
            pltpu.VMEM((tok_rows, width), jnp.float32),
            buffer(*query.shape),
            buffer(*hidden_states.shape),
            buffer(1, width),
            pltpu.SemaphoreType.DMA((6,)),
            pltpu.SemaphoreType.DMA((2, 3)),
            pltpu.SemaphoreType.DMA((2, 3)),
            pltpu.SemaphoreType.DMA((8, levels)),
            pltpu.SemaphoreType.DMA((devices,)),
        ],
        compiler_params=pltpu.CompilerParams(
            collective_id=1, has_side_effects=True, vmem_limit_bytes=56 * 1024 * 1024
        ),
    )(o_proj, query, keys, values, hidden_states, norm_gain.reshape(1, -1))


def local(
    hidden_states,
    o_proj,
    norm_gain,
    router_weight,
    routes,
    w_gate,
    w_up,
    w_down,
    query,
    keys,
    values,
):
    tok_rows = hidden_states.shape[0]
    model_width = hidden_states.shape[1]
    per_token = routes.shape[1]
    experts = router_weight.shape[1]
    devices = lax.axis_size("ctx")
    shard_count = devices // experts
    capacity = min(tok_rows, (tok_rows * per_token // experts // shard_count + 1) * shard_count)
    slots = -(-capacity // 8) * 8
    attended, stream, normed = attention_call(
        o_proj, query, keys, values, hidden_states, norm_gain
    )
    features = stream.astype(jnp.float32)
    logits = jnp.dot(normed, router_weight, preferred_element_type=jnp.float32)
    choices = jnp.arange(experts, dtype=jnp.int32)
    named = jnp.any(routes[:, :, None] == choices, axis=1)
    top_logit = jnp.max(jnp.where(named, logits, -jnp.inf), axis=-1, keepdims=True)
    raw = jnp.where(named, jnp.exp(jnp.where(named, logits - top_logit, 0.0)), 0.0)
    route_weight = raw / jnp.sum(raw, axis=-1, keepdims=True)
    tokens = jnp.arange(tok_rows, dtype=jnp.int32)
    earlier = (tokens[None, :] < tokens[:, None]).astype(jnp.bfloat16)
    rank = jnp.dot(earlier, named.astype(jnp.bfloat16), preferred_element_type=jnp.float32)
    slot_index = jnp.arange(slots, dtype=jnp.int32)
    assign = named[:, :, None] & (rank.astype(jnp.int32)[:, :, None] == slot_index)
    place = jnp.transpose(assign.astype(jnp.bfloat16), (1, 2, 0))
    summed = experts_call(
        normed, place, jnp.swapaxes(w_gate, 1, 2), jnp.swapaxes(w_up, 1, 2), w_down
    ).reshape(experts * slots, model_width)
    weights = jnp.where(assign, route_weight[:, :, None], 0.0).reshape(tok_rows, experts * slots)
    upper = weights.astype(jnp.bfloat16)
    lower = (weights - upper.astype(jnp.float32)).astype(jnp.bfloat16)
    both = jnp.dot(
        jnp.concatenate([upper, lower]), summed, preferred_element_type=jnp.float32
    )
    moe_output = (features + both[:tok_rows] + both[tok_rows:]).astype(jnp.bfloat16)
    return (moe_output, attended)


def solution(mesh):
    in_specs = (
        P(("parts", "ctx"), None),
        P("ctx", None),
        P(),
        P(),
        P(("parts", "ctx"), None),
        P("ctx", None, None),
        P("ctx", None, None),
        P("ctx", None, None),
        P(("parts", "ctx"), None),
        P(("parts", "ctx"), None),
        P(("parts", "ctx"), None),
    )
    out_specs = (P(("parts", "ctx"), None), P(("parts", "ctx"), None))
    return jax.shard_map(local, mesh=mesh, in_specs=in_specs, out_specs=out_specs, check_vma=False)
```

```python
import functools

import jax
import jax.numpy as jnp
from jax import lax
from jax.experimental import pallas as pl
from jax.experimental.pallas import tpu as pltpu
from jax.sharding import PartitionSpec as P

HEADS = 32
KV_HEADS = 4
HEAD_DIM = 64


MEMBERS = 4
AHEAD_GATHER = 2
AHEAD_EXPERTS = 2


def xor(a, b, count):
    result, bit = 0, 1
    while bit < count:
        result += (a // bit + b // bit) % 2 * bit
        bit *= 2
    return result


def expert_kernel(
    groups,
    normed_ref,
    place_ref,
    gate_hbm,
    up_hbm,
    down_hbm,
    out_ref,
    recv,
    pieces,
    near,
    pair_sum,
    far,
    final,
    gate_ref,
    up_ref,
    down_ref,
    dense,
    placed,
    cross,
    weight_sem,
    send_sem,
    recv_sem,
):
    me = lax.axis_index("ctx")
    group = me // MEMBERS
    j = me % MEMBERS
    j_sib = j + 1 - 2 * (j % 2)
    j_far = (j + 2) % MEMBERS
    j_diag = MEMBERS - 1 - j
    sibling = group * MEMBERS + j_sib
    partner = group * MEMBERS + j_far

    def to(src, dst, kind, here, there, device):
        return pltpu.make_async_remote_copy(
            src_ref=src,
            dst_ref=dst,
            send_sem=send_sem.at[kind, here],
            recv_sem=recv_sem.at[kind, there],
            device_id={"ctx": device},
            device_id_type=pl.DeviceIdType.MESH,
        )

    weight_copies = [
        pltpu.make_async_copy(src, dst, weight_sem.at[i])
        for i, (src, dst) in enumerate(
            ((gate_hbm.at[0], gate_ref), (up_hbm.at[0], up_ref), (down_hbm.at[0], down_ref))
        )
    ]
    for copy in weight_copies:
        copy.start()

    barrier = pltpu.get_barrier_semaphore()

    def greet(device):
        pl.semaphore_signal(
            barrier, inc=1, device_id={"ctx": device}, device_id_type=pl.DeviceIdType.MESH
        )

    @pl.loop(1, groups)
    def _(o):
        greet(lax.rem(group + o, groups) * MEMBERS + j)

    greet(sibling)
    greet(partner)
    pl.semaphore_wait(barrier, groups + 1)

    levels = groups // 2
    level, row = group // 2, group % 2

    def whole(kind, src, dst, at, there):
        return to(src, dst, kind, at, there, (at * 2 + row) * MEMBERS + j)

    def send_block(at):
        return (
            whole(0, normed_ref, dense.at[level], at, level),
            whole(8, place_ref.at[pl.ds(at * 2, 2)], placed.at[level], at, level),
        )

    def block_arrived(at):
        return (
            whole(0, normed_ref, dense.at[at], at, at),
            whole(8, place_ref.at[pl.ds(at * 2, 2)], placed.at[at], at, at),
        )

    def send_cross(at):
        return to(
            cross.at[at],
            recv.at[at * 2 + row, j],
            9,
            at,
            at,
            (level * 2 + 1 - row) * MEMBERS + j,
        )

    def level_at(step):
        return xor(level, step, levels)

    def share_sibling(s):
        return to(recv.at[s, j], recv.at[s, j], 1, s, s, sibling)

    def share_partner(s):
        return to(recv.at[s, j], recv.at[s, j], 2, s, s, partner)

    def share_diag(s):
        return to(recv.at[s, j_far], recv.at[s, j_far], 3, s, s, sibling)

    def piece_near(s):
        return to(pieces.at[s, j_sib], near.at[s, 0], 4, s, s, sibling)

    def piece_diag(s):
        return to(pieces.at[s, j_diag], near.at[s, 1], 5, s, s, sibling)

    def piece_far(s):
        return to(pair_sum.at[s], far.at[s], 6, s, s, partner)

    def give_back(s):
        return to(final.at[s], out_ref.at[group], 7, s, group, s * MEMBERS + j)

    def given_back(s):
        return to(final.at[s], out_ref.at[s], 7, s, s, s * MEMBERS + j)

    def source(step):
        return xor(group, step, groups)

    @pl.loop(1, min(AHEAD_EXPERTS + 1, levels))
    def _(o):
        for copy in send_block(level_at(o)):
            copy.start()

    dense[level] = normed_ref[...]
    placed[level] = place_ref[pl.ds(level * 2, 2)]

    rows, width = recv.shape[2], recv.shape[3]

    @pl.loop(0, groups + 4)
    def _(t):
        @pl.when((t >= 4) & (t < groups + 4))
        def _():
            s = source(t - 4)
            piece_far(s).wait_recv()
            total = (
                pieces[s, j].astype(jnp.float32)
                + near[s, 0].astype(jnp.float32)
                + far[s].astype(jnp.float32)
            ).astype(jnp.bfloat16)

            @pl.when(t == 4)
            def _():
                out_ref[group] = total

            @pl.when(t > 4)
            def _():
                final[s] = total
                give_back(s).start()

        @pl.when((t >= 3) & (t < groups + 3))
        def _():
            s = source(t - 3)
            piece_near(s).wait_recv()
            piece_diag(s).wait_recv()
            pair_sum[s] = (
                pieces[s, j_far].astype(jnp.float32) + near[s, 1].astype(jnp.float32)
            ).astype(jnp.bfloat16)
            piece_far(s).start()

        @pl.when(t < groups)
        def _():
            s = source(t)

            at = s // 2

            @pl.when(t % 2 == 0)
            def _():
                @pl.when(t > 0)
                def _():
                    for copy in block_arrived(at):
                        copy.wait_recv()

                @pl.when((t > 0) & (t // 2 + AHEAD_EXPERTS < levels))
                def _():
                    for copy in send_block(level_at(t // 2 + AHEAD_EXPERTS)):
                        copy.start()

                cross[at] = jnp.dot(
                    placed[at, 1 - row], dense[at], preferred_element_type=jnp.float32
                ).astype(jnp.bfloat16)
                send_cross(at).start()
                recv[s, j] = jnp.dot(
                    placed[at, row], dense[at], preferred_element_type=jnp.float32
                ).astype(jnp.bfloat16)

            @pl.when(t % 2 == 1)
            def _():
                send_cross(at).wait_recv()

            share_partner(s).start()
            share_sibling(s).start()

        @pl.when((t >= 1) & (t < groups + 1))
        def _():
            s = source(t - 1)
            share_partner(s).wait_recv()
            share_diag(s).start()

        @pl.when((t >= 2) & (t < groups + 2))
        def _():
            s = source(t - 2)

            @pl.when(t == 2)
            def _():
                for copy in weight_copies:
                    copy.wait()

            share_sibling(s).wait_recv()
            share_diag(s).wait_recv()
            block = recv[s].reshape(MEMBERS * rows, width)
            across = (((1,), (1,)), ((), ()))
            gate = lax.dot_general(
                block, gate_ref[...], across, preferred_element_type=jnp.float32
            )
            up = lax.dot_general(block, up_ref[...], across, preferred_element_type=jnp.float32)
            activated = ((up + 1.0) * gate * jax.nn.sigmoid(1.702 * gate)).astype(jnp.bfloat16)
            for at in range(0, width, 768):
                span = slice(at, min(at + 768, width))
                piece = jnp.dot(
                    activated, down_ref[:, span], preferred_element_type=jnp.float32
                ).astype(jnp.bfloat16)
                pieces[s, :, :, span] = piece.reshape(MEMBERS, rows, span.stop - span.start)
            piece_near(s).start()
            piece_diag(s).start()

    @pl.loop(0, groups)
    def _(s):
        share_sibling(s).wait_send()
        share_partner(s).wait_send()
        share_diag(s).wait_send()
        piece_near(s).wait_send()
        piece_diag(s).wait_send()
        piece_far(s).wait_send()

    @pl.loop(0, levels)
    def _(at):
        send_cross(at).wait_send()

    @pl.loop(1, levels)
    def _(o):
        for copy in send_block(level_at(o)):
            copy.wait_send()

    @pl.loop(1, groups)
    def _(o):
        s = source(o)
        given_back(s).wait_send()
        given_back(s).wait_recv()


def experts_call(normed, place, w_gate, w_up, w_down):
    groups, slots, tok_rows = place.shape
    width = normed.shape[1]
    hidden = w_gate.shape[1]
    anywhere = pl.BlockSpec(memory_space=pl.ANY)
    vmem = pl.BlockSpec(memory_space=pltpu.VMEM)

    def buffer(*shape):
        return pltpu.VMEM(shape, jnp.bfloat16)

    return pl.pallas_call(
        functools.partial(expert_kernel, groups),
        out_shape=jax.ShapeDtypeStruct((groups, slots, width), jnp.bfloat16),
        in_specs=[vmem, vmem, anywhere, anywhere, anywhere],
        out_specs=vmem,
        scratch_shapes=[
            buffer(groups, MEMBERS, slots, width),
            buffer(groups, MEMBERS, slots, width),
            buffer(groups, 2, slots, width),
            buffer(groups, slots, width),
            buffer(groups, slots, width),
            buffer(groups, slots, width),
            buffer(hidden, width),
            buffer(hidden, width),
            buffer(hidden, width),
            buffer(groups // 2, tok_rows, width),
            buffer(groups // 2, 2, slots, tok_rows),
            buffer(groups // 2, slots, width),
            pltpu.SemaphoreType.DMA((3,)),
            pltpu.SemaphoreType.DMA((10, groups)),
            pltpu.SemaphoreType.DMA((10, groups)),
        ],
        compiler_params=pltpu.CompilerParams(
            collective_id=0, has_side_effects=True, vmem_limit_bytes=56 * 1024 * 1024
        ),
    )(normed, place, w_gate, w_up, w_down)


def attention_kernel(
    levels,
    wo_hbm,
    query_hbm,
    keys_hbm,
    values_hbm,
    hidden_hbm,
    gain_hbm,
    attended_ref,
    stream_ref,
    normed_ref,
    wo,
    key_window,
    value_window,
    mixed,
    total,
    query_ref,
    hidden_ref,
    gain_ref,
    load_sem,
    kv_send,
    kv_recv,
    send_sem,
    recv_sem,
):
    count = levels * 8
    me = lax.axis_index("ctx")
    level = me // 8
    row = (me // 4) % 2
    column = (me // 2) % 2
    core = me % 2
    sibling = me + 1 - 2 * core

    def place(at, first, second):
        down = first * (1 - core) + second * core
        over = first * core + second * (1 - core)
        return (
            (at * 2 + row + down * (1 - 2 * row)) * 4
            + (column + over * (1 - 2 * column)) * 2
            + core
        )

    def send(slot, kind, index, device):
        return pltpu.make_async_remote_copy(
            src_ref=wo.at[slot],
            dst_ref=wo.at[slot],
            send_sem=send_sem.at[kind, index],
            recv_sem=recv_sem.at[slot],
            device_id={"ctx": device},
            device_id_type=pl.DeviceIdType.MESH,
        )

    loads = [
        pltpu.make_async_copy(src, dst, load_sem.at[i])
        for i, (src, dst) in enumerate(
            (
                (wo_hbm, wo.at[me]),
                (keys_hbm, key_window.at[3]),
                (values_hbm, value_window.at[3]),
                (query_hbm, query_ref),
                (hidden_hbm, hidden_ref),
                (gain_hbm, gain_ref),
            )
        )
    ]
    for load in loads:
        load.start()
    across, beyond = place(level, 1, 0), place(level, 0, 1)

    def level_at(step):
        return xor(level, step, levels)

    def along(at):
        return send(me, 0, at, place(at, 0, 0))

    def to_first(at):
        return send(place(at, 0, 0), 1, at, across)

    def to_second(at, first):
        return send(place(at, first, 0), 2 + first, at, beyond)

    def to_sibling(at, first, second):
        return send(place(at, first, second), 4 + 2 * first + second, at, sibling)

    def arrived(slot):
        send(slot, 0, 0, sibling).wait_recv()

    def kv_copy(part, distance):
        target = (key_window, value_window)[part]
        return pltpu.make_async_remote_copy(
            src_ref=target.at[3],
            dst_ref=target.at[3 - distance],
            send_sem=kv_send.at[part, distance - 1],
            recv_sem=kv_recv.at[part, distance - 1],
            device_id={"ctx": lax.rem(me + distance, count)},
            device_id_type=pl.DeviceIdType.MESH,
        )

    barrier = pltpu.get_barrier_semaphore()

    def greet(device):
        pl.semaphore_signal(
            barrier, inc=1, device_id={"ctx": device}, device_id_type=pl.DeviceIdType.MESH
        )

    @pl.loop(1, levels)
    def _(o):
        greet(place(lax.rem(level + o, levels), 0, 0))

    for device in (sibling, across, beyond):
        greet(device)
    for distance in (1, 2, 3):
        greet(lax.rem(me + distance, count))
        greet(lax.rem(me - distance + count, count))
    for load in loads[:3]:
        load.wait()
    pl.semaphore_wait(barrier, levels - 1 + 9)

    for distance in (1, 2, 3):
        for part in (0, 1):
            kv_copy(part, distance).start()

    @pl.loop(1, min(AHEAD_GATHER + 1, levels))
    def _(o):
        along(level_at(o)).start()

    total[...] = jnp.zeros_like(total)
    for load in loads[3:]:
        load.wait()
    tok_rows = query_ref.shape[0]
    window = 4 * tok_rows
    width = total.shape[1]
    block_rows = wo.shape[1]
    group_size = HEADS // KV_HEADS
    chunk = group_size * HEAD_DIM

    def attend(g):
        pair = pl.ds(pl.multiple_of(g // 2 * 2 * HEAD_DIM, 2 * HEAD_DIM), 2 * HEAD_DIM)
        even = g % 2 == 0
        key_pair = key_window[:, :, pair].reshape(window, 2 * HEAD_DIM)
        value_pair = value_window[:, :, pair].reshape(window, 2 * HEAD_DIM)
        head_keys = jnp.where(even, key_pair[:, :HEAD_DIM], key_pair[:, HEAD_DIM:])
        head_values = jnp.where(even, value_pair[:, :HEAD_DIM], value_pair[:, HEAD_DIM:])
        at = pl.ds(pl.multiple_of(g * chunk, chunk), chunk)
        queries = query_ref[:, at]
        query_pos = lax.broadcasted_iota(jnp.int32, (tok_rows, window), 0)
        key_pos = lax.broadcasted_iota(jnp.int32, (tok_rows, window), 1) - 3 * tok_rows
        allowed = (key_pos <= query_pos) & (key_pos + me * tok_rows >= 0)
        for h in range(group_size):
            lanes = slice(h * HEAD_DIM, (h + 1) * HEAD_DIM)
            scores = lax.dot_general(
                queries[:, lanes],
                head_keys,
                (((1,), (1,)), ((), ())),
                preferred_element_type=jnp.float32,
            ) * HEAD_DIM ** (-0.5)
            scores = jnp.where(allowed, scores, -1e30)
            top_score = jnp.max(scores, axis=-1, keepdims=True)
            weights = jnp.where(allowed, jnp.exp(scores - top_score), 0.0)
            probs = weights * (1.0 / jnp.sum(weights, axis=-1, keepdims=True))
            mixed[:, lanes] = jnp.dot(
                probs.astype(jnp.bfloat16), head_values, preferred_element_type=jnp.float32
            ).astype(jnp.bfloat16)
        attended_ref[:, at] = mixed[...]

    @pl.loop(0, levels + 3)
    def _(t):
        @pl.when(t < levels)
        def _():
            at = level_at(t)

            @pl.when(t > 0)
            def _():
                arrived(place(at, 0, 0))

            to_first(at).start()
            to_second(at, 0).start()

            @pl.when((t > 0) & (t + AHEAD_GATHER < levels))
            def _():
                along(level_at(t + AHEAD_GATHER)).start()

            to_sibling(at, 0, 0).start()

        @pl.when(t == 0)
        def _():
            for distance in (1, 2, 3):
                for part in (0, 1):
                    kv_copy(part, distance).wait_recv()

        @pl.when((t >= 1) & (t < levels + 1))
        def _():
            at = level_at(t - 1)
            arrived(place(at, 1, 0))
            to_second(at, 1).start()
            to_sibling(at, 1, 0).start()

        @pl.when(t < KV_HEADS)
        def _():
            attend(t)

        @pl.when((t >= 2) & (t < levels + 2))
        def _():
            at = level_at(t - 2)
            for first in (0, 1):
                arrived(place(at, first, 1))
                to_sibling(at, first, 1).start()

        @pl.when(t >= 3)
        def _():
            at = level_at(t - 3)
            for group in (at * 2, at * 2 + 1):
                for member in (0, 2):
                    arrived(group * 4 + member + 1 - core)
                depth = 4 * block_rows
                rows = wo[pl.ds(group * 4, 4)].reshape(depth, width)
                heads = attended_ref[:, pl.ds(pl.multiple_of(group * depth, depth), depth)]
                for start in range(0, width, 768):
                    span = slice(start, min(start + 768, width))
                    total[:, span] += jnp.dot(
                        heads, rows[:, span], preferred_element_type=jnp.float32
                    )

    stream = (hidden_ref[...].astype(jnp.float32) + total[...]).astype(jnp.bfloat16)
    stream_ref[...] = stream
    features = stream.astype(jnp.float32)
    normed_ref[...] = (
        features
        * lax.rsqrt(jnp.mean(features * features, axis=-1, keepdims=True) + 1e-05)
        * gain_ref[...].astype(jnp.float32)
    ).astype(jnp.bfloat16)

    @pl.loop(0, levels)
    def _(at):
        to_first(at).wait_send()
        for first in (0, 1):
            to_second(at, first).wait_send()
            for second in (0, 1):
                to_sibling(at, first, second).wait_send()

    @pl.loop(1, levels)
    def _(o):
        along(lax.rem(level + o, levels)).wait_send()

    for distance in (1, 2, 3):
        for part in (0, 1):
            kv_copy(part, distance).wait_send()


def attention_call(o_proj, query, keys, values, hidden_states, norm_gain):
    devices = lax.axis_size("ctx")
    levels = devices // 8
    block_rows, width = o_proj.shape
    tok_rows = query.shape[0]

    def buffer(*shape):
        return pltpu.VMEM(shape, jnp.bfloat16)

    return pl.pallas_call(
        functools.partial(attention_kernel, levels),
        out_shape=[
            jax.ShapeDtypeStruct(query.shape, jnp.bfloat16),
            jax.ShapeDtypeStruct(hidden_states.shape, jnp.bfloat16),
            jax.ShapeDtypeStruct(hidden_states.shape, jnp.bfloat16),
        ],
        in_specs=[pl.BlockSpec(memory_space=pl.ANY)] * 6,
        out_specs=[pl.BlockSpec(memory_space=pltpu.VMEM)] * 3,
        scratch_shapes=[
            buffer(devices, block_rows, width),
            buffer(4, tok_rows, keys.shape[1]),
            buffer(4, tok_rows, keys.shape[1]),
            buffer(tok_rows, HEADS // KV_HEADS * HEAD_DIM),
            pltpu.VMEM((tok_rows, width), jnp.float32),
            buffer(*query.shape),
            buffer(*hidden_states.shape),
            buffer(1, width),
            pltpu.SemaphoreType.DMA((6,)),
            pltpu.SemaphoreType.DMA((2, 3)),
            pltpu.SemaphoreType.DMA((2, 3)),
            pltpu.SemaphoreType.DMA((8, levels)),
            pltpu.SemaphoreType.DMA((devices,)),
        ],
        compiler_params=pltpu.CompilerParams(
            collective_id=1, has_side_effects=True, vmem_limit_bytes=56 * 1024 * 1024
        ),
    )(o_proj, query, keys, values, hidden_states, norm_gain.reshape(1, -1))


def local(
    hidden_states,
    o_proj,
    norm_gain,
    router_weight,
    routes,
    w_gate,
    w_up,
    w_down,
    query,
    keys,
    values,
):
    tok_rows = hidden_states.shape[0]
    model_width = hidden_states.shape[1]
    per_token = routes.shape[1]
    experts = router_weight.shape[1]
    devices = lax.axis_size("ctx")
    shard_count = devices // experts
    capacity = min(tok_rows, (tok_rows * per_token // experts // shard_count + 1) * shard_count)
    slots = -(-capacity // 8) * 8
    attended, stream, normed = attention_call(
        o_proj, query, keys, values, hidden_states, norm_gain
    )
    features = stream.astype(jnp.float32)
    logits = jnp.dot(normed, router_weight, preferred_element_type=jnp.float32)
    choices = jnp.arange(experts, dtype=jnp.int32)
    named = jnp.any(routes[:, :, None] == choices, axis=1)
    top_logit = jnp.max(jnp.where(named, logits, -jnp.inf), axis=-1, keepdims=True)
    raw = jnp.where(named, jnp.exp(jnp.where(named, logits - top_logit, 0.0)), 0.0)
    route_weight = raw / jnp.sum(raw, axis=-1, keepdims=True)
    tokens = jnp.arange(tok_rows, dtype=jnp.int32)
    earlier = (tokens[None, :] < tokens[:, None]).astype(jnp.bfloat16)
    rank = jnp.dot(earlier, named.astype(jnp.bfloat16), preferred_element_type=jnp.float32)
    slot_index = jnp.arange(slots, dtype=jnp.int32)
    assign = named[:, :, None] & (rank.astype(jnp.int32)[:, :, None] == slot_index)
    place = jnp.transpose(assign.astype(jnp.bfloat16), (1, 2, 0))
    summed = experts_call(
        normed, place, jnp.swapaxes(w_gate, 1, 2), jnp.swapaxes(w_up, 1, 2), w_down
    ).reshape(experts * slots, model_width)
    weights = jnp.where(assign, route_weight[:, :, None], 0.0).reshape(tok_rows, experts * slots)
    upper = weights.astype(jnp.bfloat16)
    lower = (weights - upper.astype(jnp.float32)).astype(jnp.bfloat16)
    both = jnp.dot(
        jnp.concatenate([upper, lower]), summed, preferred_element_type=jnp.float32
    )
    moe_output = (features + both[:tok_rows] + both[tok_rows:]).astype(jnp.bfloat16)
    return (moe_output, attended)


def solution(mesh):
    in_specs = (
        P(("parts", "ctx"), None),
        P("ctx", None),
        P(),
        P(),
        P(("parts", "ctx"), None),
        P("ctx", None, None),
        P("ctx", None, None),
        P("ctx", None, None),
        P(("parts", "ctx"), None),
        P(("parts", "ctx"), None),
        P(("parts", "ctx"), None),
    )
    out_specs = (P(("parts", "ctx"), None), P(("parts", "ctx"), None))
    return jax.shard_map(local, mesh=mesh, in_specs=in_specs, out_specs=out_specs, check_vma=False)
```
